128 devices in a mesh: grp: 8 (over y, core), ingrp: 16 (over x, z).
Axes of the slice: x: 4, y: 4, z: 4, core: 2. Of those that a mesh axis runs over, the one named last changes fastest.
Arguments:
- tokens: bfloat16 [16384, 3584], P(('grp', 'ingrp')), may hold values from -6 to 6
- out_grad: bfloat16 [16384, 3584], P(('grp', 'ingrp')), may hold values from -1.5 to 1.5
- route_weights: bfloat16 [16384, 4], P(('grp', 'ingrp')), may hold values from 0.049804688 to 0.59765625
- expert_ids: int32 [16384, 4], P(('grp', 'ingrp')), may hold values from 0 to 127, as said below
- w_gate: bfloat16 [128, 3584, 1024], P(('grp', 'ingrp')), may hold values from -0.09375 to 0.09375
- w_up: bfloat16 [128, 3584, 1024], P(('grp', 'ingrp')), may hold values from -0.09375 to 0.09375
- w_down: bfloat16 [128, 1024, 3584], P(('grp', 'ingrp')), may hold values from -0.1875 to 0.1875
Outputs:
- x_grad: bfloat16 [16384, 3584], P(('grp', 'ingrp'))
- route_grad: float32 [16384, 4], P(('grp', 'ingrp'))
The draws below stay inside these ranges and needn't reach their ends.
Inputs may be any that keep to these rules, and one draw needn't show every extreme that they name: `expert_ids`: each token names 4 distinct experts in 2 distinct node groups, 2 in each; expert e lies in group e // 16, and ids k and k + 1 with k even lie in one group. Of each device's tokens every group is chosen by exactly 32, and at most 8 name any one expert; in every draw one and the same expert of each group is named by exactly 8 tokens of every device, so that expert receives 1024 rows in all.
All inputs are finite; a program needn't handle non-finite values.
Results may differ from the reference program's by a relative error of at most 0.0049.
Values may be sent and summed in bfloat16 or wider, within the bound.
No kernel may reach another device: no remote copies, remote signals or barrier semaphores. Data moves between devices by JAX's collectives and lax.ppermute only.
A program may use at most 128 MiB of HBM per device.

```python
import jax
import jax.numpy as jnp
from jax import lax

D = 3584
FF = 1024
TOP = 4
GSEL = 2
TOK_DEV = 128
GROUPS = 8
MEMBERS = 16
EXPERTS = 128
TOKENS = 16384
CAP = 8


def route_table(key):
    blocks = TOKENS // TOK_DEV
    key_perm, key_order, key_hot = jax.random.split(key, 3)
    scores = jax.random.randint(key_perm, (blocks, TOK_DEV), 0, 1 << 16) * TOK_DEV + jnp.arange(TOK_DEV, dtype=jnp.int32)[None, :]
    permuted = jnp.argsort(scores, axis=1).astype(jnp.int32)
    first_group = permuted % GROUPS
    second_rank = permuted // GROUPS
    second_group = (first_group + 1 + second_rank % (GROUPS - 1)) % GROUPS
    half_span = TOK_DEV // GROUPS
    span = 2 * half_span
    rest_load = TOP * TOK_DEV // GROUPS - CAP
    base_load = rest_load // (MEMBERS - 1)
    extra_load = rest_load % (MEMBERS - 1)
    other_loads = base_load + (jnp.arange(MEMBERS - 1, dtype=jnp.int32) < extra_load).astype(jnp.int32)
    loads = jnp.concatenate([jnp.full((1,), CAP, jnp.int32), other_loads])
    load_ends = jnp.cumsum(loads)
    order_scores = jax.random.randint(key_order, (blocks, GROUPS, MEMBERS), 0, 1 << 16) * MEMBERS + jnp.arange(MEMBERS, dtype=jnp.int32)
    order_scores = order_scores.at[:, :, 0].set(-1)
    member_order = jnp.argsort(order_scores, axis=2).astype(jnp.int32)
    hot_member = jax.random.randint(key_hot, (GROUPS,), 0, MEMBERS)
    block_index = jnp.arange(blocks, dtype=jnp.int32)[:, None]

    def member_of(group, rank, offset):
        layout = rank + offset * span
        position = jnp.sum((layout[..., None] >= load_ends).astype(jnp.int32), axis=-1)
        shuffled = member_order[block_index, group, position]
        return group * MEMBERS + (hot_member[group] + shuffled) % MEMBERS
    columns = []
    for offset in range(TOP // GSEL):
        columns.append(member_of(first_group, second_rank, offset))
    for offset in range(TOP // GSEL):
        columns.append(member_of(second_group, half_span + second_rank, offset))
    chosen = jnp.stack(columns, axis=-1)
    return chosen.reshape(TOKENS, TOP).astype(jnp.int32)


def draw_expert_ids(key, part):
    key = jax.random.fold_in(key, 11)
    return route_table(key)


def block_levels(rng, dims, pieces, low, top_value):
    def one(dim, parts):
        steps = jax.random.uniform(jax.random.fold_in(jax.random.fold_in(rng, 6), dim), (parts,), jnp.float32, low / len(pieces), top_value / len(pieces))
        return jnp.repeat(jnp.exp(steps), dims[dim] // parts).reshape((-1,) + (1,) * (len(dims) - dim - 1))

    factor_of = one(*pieces[0])
    for cut in pieces[1:]:
        factor_of = factor_of * one(*cut)
    return factor_of


def normal_values(key, dims, deviation, reach, pieces=(), held_as=jnp.bfloat16):
    drawn = deviation * jax.random.normal(key, dims, jnp.float32)
    if pieces:
        drawn = drawn * block_levels(key, dims, pieces, -0.22, 0.18)
    return jnp.clip(drawn, -reach, reach).astype(held_as)


def setup_inputs(seed: int = 0) -> dict:
    splits = jax.random.split(jax.random.key(seed), 8)
    return {
        "tokens": normal_values(splits[0], (TOKENS, D), 1.0, 6.0, ((0, 128),)),
        "out_grad": normal_values(splits[1], (TOKENS, D), 0.25, 1.5, ((0, 128),)),
        "route_weights": jnp.clip(0.049804688 + 0.54785156 * jax.random.uniform(splits[2], (TOKENS, TOP), jnp.float32) ** block_levels(splits[2], (TOKENS, TOP), ((0, 128),), -0.2, 0.2), 0.049804688, 0.59765625).astype(jnp.bfloat16),
        "expert_ids": draw_expert_ids(jax.random.fold_in(splits[7], 71), 0),
        "w_gate": normal_values(splits[4], (EXPERTS, D, FF), D ** -0.5, 0.09375, ((0, 128),)),
        "w_up": normal_values(splits[5], (EXPERTS, D, FF), D ** -0.5, 0.09375, ((0, 128),)),
        "w_down": normal_values(splits[6], (EXPERTS, FF, D), FF ** -0.5, 0.1875, ((0, 128),)),
    }


def expert_rows(rows_x, rows_dy, rows_w, gate_mat, up_mat, down_mat):
    gate = jnp.dot(rows_x, gate_mat, preferred_element_type=jnp.float32)
    upper = jnp.dot(rows_x, up_mat, preferred_element_type=jnp.float32)
    sigma = jax.nn.sigmoid(gate)
    active = gate * sigma
    hidden = active * upper
    raw_grad = lax.dot_general(rows_dy, down_mat, (((1,), (1,)), ((), ())), preferred_element_type=jnp.float32)
    route_part = jnp.sum(raw_grad * hidden, axis=1)
    hidden_grad = rows_w[:, None] * raw_grad
    d_gate = (hidden_grad * upper * sigma * (1.0 + gate * (1.0 - sigma))).astype(jnp.bfloat16)
    d_upper = (hidden_grad * active).astype(jnp.bfloat16)
    contrib = lax.dot_general(d_gate, gate_mat, (((1,), (1,)), ((), ())), preferred_element_type=jnp.float32)
    contrib = contrib + lax.dot_general(d_upper, up_mat, (((1,), (1,)), ((), ())), preferred_element_type=jnp.float32)
    return contrib, route_part


def reference(tokens, out_grad, route_weights, expert_ids, w_gate, w_up, w_down):
    row_limit = (TOKENS // TOK_DEV) * CAP
    weights_wide = route_weights.astype(jnp.float32)

    def per_expert(carry, inputs):
        grad_acc, route_acc = carry
        expert, gate_mat, up_mat, down_mat = inputs
        chosen_pair = expert_ids == expert
        chosen = jnp.any(chosen_pair, axis=1)
        position = jnp.cumsum(chosen.astype(jnp.int32)) - 1
        target = jnp.where(chosen, position, row_limit).astype(jnp.int32)
        row_index = jnp.full((row_limit,), TOKENS, jnp.int32).at[target].set(jnp.arange(TOKENS, dtype=jnp.int32), mode="drop")
        valid = row_index < TOKENS
        row_index = jnp.minimum(row_index, TOKENS - 1)
        weight_tok = jnp.sum(jnp.where(chosen_pair, weights_wide, jnp.zeros((), jnp.float32)), axis=1)
        weight_row = jnp.where(valid, weight_tok[row_index], jnp.zeros((), jnp.float32))
        contrib, route_part = expert_rows(tokens[row_index], out_grad[row_index], weight_row, gate_mat, up_mat, down_mat)
        grad_acc = grad_acc.at[row_index].add(contrib)
        route_tok = jnp.zeros((TOKENS,), jnp.float32).at[row_index].add(jnp.where(valid, route_part, jnp.zeros((), jnp.float32)))
        route_acc = route_acc + jnp.where(chosen_pair, route_tok[:, None], jnp.zeros((), jnp.float32))
        return (grad_acc, route_acc), None

    start = (jnp.zeros((TOKENS, D), jnp.float32), jnp.zeros((TOKENS, TOP), jnp.float32))
    experts_all = jnp.arange(EXPERTS, dtype=jnp.int32)
    (grad_acc, route_acc), unused = lax.scan(per_expert, start, (experts_all, w_gate, w_up, w_down))
    return grad_acc.astype(jnp.bfloat16), route_acc
```

```python
import jax
import jax.numpy as jnp
from jax import lax
from jax.sharding import PartitionSpec as P

BOTH = ("grp", "ingrp")


def matmul(left, right, kind=jnp.bfloat16):
    return jnp.dot(left, right, preferred_element_type=jnp.float32).astype(kind)


def matmul_t(left, right):
    return lax.dot_general(
        left, right, (((1,), (1,)), ((), ())), preferred_element_type=jnp.float32
    )


def exchange(rows, experts):
    parts = rows.reshape((experts, -1) + rows.shape[1:])
    return lax.all_to_all(parts, BOTH, split_axis=0, concat_axis=0, tiled=True).reshape(rows.shape)


def local(tokens, out_grad, route_weights, expert_ids, w_gate, w_up, w_down):
    tok_rows, width = tokens.shape
    top = expert_ids.shape[1]
    experts = lax.axis_size("grp") * lax.axis_size("ingrp")
    capacity = 2 * tok_rows * top // experts
    slot_total = experts * capacity
    pair_total = tok_rows * top
    gate_mat, up_mat, down_mat = w_gate[0], w_up[0], w_down[0]

    pair_ids = expert_ids.reshape(-1)
    onehot = pair_ids[:, None] == jnp.arange(experts, dtype=jnp.int32)[None, :]
    earlier = (
        jnp.arange(pair_total, dtype=jnp.int32)[:, None]
        > jnp.arange(pair_total, dtype=jnp.int32)[None, :]
    )
    before = matmul(earlier.astype(jnp.bfloat16), onehot.astype(jnp.bfloat16), jnp.float32)
    ranks = jnp.sum(jnp.where(onehot, before, 0.0), axis=1).astype(jnp.int32)
    slots = (pair_ids * capacity + ranks).reshape(tok_rows, top)

    slot_iota = jnp.arange(slot_total, dtype=jnp.int32)
    taken = slots[:, :, None] == slot_iota[None, None, :]
    pick = jnp.any(taken, axis=1).astype(jnp.bfloat16)
    spread = lambda rows: lax.dot_general(
        pick, rows, (((0,), (0,)), ((), ())), preferred_element_type=jnp.float32
    ).astype(jnp.bfloat16)

    rows_x = exchange(spread(tokens), experts)
    rows_dy = exchange(spread(out_grad), experts)

    gate = matmul(rows_x, gate_mat, jnp.float32)
    upper = matmul(rows_x, up_mat, jnp.float32)
    sigma = jax.nn.sigmoid(gate)
    active = gate * sigma
    slope = upper * sigma * (1.0 + gate * (1.0 - sigma))
    raw = matmul_t(rows_dy, down_mat)
    route_part = jnp.sum(raw * (active * upper), axis=1)
    d_gate = (raw * slope).astype(jnp.bfloat16)
    d_upper = (raw * active).astype(jnp.bfloat16)
    contrib = (matmul_t(d_gate, gate_mat) + matmul_t(d_upper, up_mat)).astype(jnp.bfloat16)

    back_routes = exchange(route_part, experts)
    back = exchange(contrib, experts)

    weights = jnp.sum(
        jnp.where(taken, route_weights[:, :, None], jnp.zeros((), jnp.bfloat16)), axis=1
    )
    x_grad = matmul(weights, back)
    route_grad = jnp.sum(jnp.where(taken, back_routes[None, None, :], 0.0), axis=2)
    return (x_grad, route_grad)


def solution(mesh):
    return jax.shard_map(
        local,
        mesh=mesh,
        in_specs=(
            P(BOTH, None),
            P(BOTH, None),
            P(BOTH, None),
            P(BOTH, None),
            P(BOTH, None, None),
            P(BOTH, None, None),
            P(BOTH, None, None),
        ),
        out_specs=(P(BOTH, None), P(BOTH, None)),
        check_vma=False,
    )
```

```python
import functools

import jax
import jax.numpy as jnp
from jax import lax
from jax.experimental import pallas as pl
from jax.experimental.pallas import tpu as pltpu
from jax.sharding import Mesh, PartitionSpec as P

ALL = ("y", "core", "ingrp")
LIKE = ("y", "ingrp")
SIDE = 4
LANES = 128
BF16 = jnp.bfloat16
F32 = jnp.float32
VMEM_LIMIT = 56 * 1024 * 1024
LITTLE = pl.CostEstimate(flops=1024, bytes_accessed=1024, transcendentals=0)


def params():
    return pltpu.CompilerParams(vmem_limit_bytes=VMEM_LIMIT)


def div(value, size):
    return lax.shift_right_logical(value, size.bit_length() - 1)


def mod(value, size):
    return value & (size - 1)


def whole():
    return pl.BlockSpec(memory_space=pltpu.VMEM)


def dot(left, right):
    return jnp.dot(left, right, preferred_element_type=F32)


def dot_t(left, right):
    return lax.dot_general(left, right, (((1,), (1,)), ((), ())), preferred_element_type=F32)


def dot_tl(left, right):
    return lax.dot_general(left, right, (((0,), (0,)), ((), ())), preferred_element_type=F32)


def exchange(rows, axes):
    count = lax.axis_size(axes)
    parts = rows.reshape((count, -1) + rows.shape[1:])
    return lax.all_to_all(parts, axes, split_axis=0, concat_axis=0, tiled=True).reshape(rows.shape)


def swap(rows):
    return lax.ppermute(rows, "core", [(0, 1), (1, 0)])


def shift(rows, axis, step):
    def target(index):
        place = [index // SIDE, index % SIDE]
        place[axis] = (place[axis] + step) % SIDE
        return place[0] * SIDE + place[1]

    return lax.ppermute(rows, "ingrp", [(i, target(i)) for i in range(SIDE * SIDE)])


def shift_y(rows, step):
    return lax.ppermute(rows, "y", [(i, (i + step) % SIDE) for i in range(SIDE)])


def short_gather(rows, axis):
    return rows, shift(rows, axis, 1), shift(rows, axis, 2), shift(rows, axis, -1)


def near_gather(rows, axis):
    return rows, shift(rows, axis, 1), shift(rows, axis, -1)


def far_gather(near, axis, cut):
    rows, below, above = near
    return [rows, below, shift(below[:, :cut], axis, 1), shift(above[:, cut:], axis, -1), above]


def fold_body(cut, *refs):
    for half in range(2):
        below, above, low, high = refs[4 * half : 4 * half + 4]
        out_below, out_above = refs[8 + 2 * half : 10 + 2 * half]
        out_below[:, :cut] = below[:, :cut] + low[...]
        out_below[:, cut:] = below[:, cut:]
        out_above[:, :cut] = above[:, :cut]
        out_above[:, cut:] = above[:, cut:] + high[...]


def fold_far(pieces, axes, cut):
    operands = []
    for (own, below, far_low, far_high, above), axis in zip(pieces, axes):
        operands += [below, above, shift(far_low, axis, -1), shift(far_high, axis, 1)]
    shape = jax.ShapeDtypeStruct(operands[0].shape, BF16)
    out = pl.pallas_call(
        functools.partial(fold_body, cut),
        out_shape=(shape,) * 4,
        in_specs=[whole()] * 8,
        out_specs=tuple([whole()] * 4),
        compiler_params=params(),
        name="fold_far",
    )(*operands)
    return (pieces[0][0], *out[:2]), (pieces[1][0], *out[2:])


def fold_near(pieces, axis):
    own, below, above = pieces
    return own, shift(below, axis, -1), shift(above, axis, 1)


def put_pieces(out, start, pieces, cut):
    size = pieces[0].shape[0]
    own, below, far_low, far_high, above = pieces
    out[start : start + size, :] = own[...]
    out[start + size : start + 2 * size, :] = below[...]
    out[start + 2 * size : start + 3 * size, :cut] = far_low[...]
    out[start + 2 * size : start + 3 * size, cut:] = far_high[...]
    out[start + 3 * size : start + 4 * size, :] = above[...]


def piece_shapes(size, width, cut):
    cols = [width, width, cut, width - cut, width]
    return [jax.ShapeDtypeStruct((size, c), BF16) for c in cols]


def pack_body(*refs):
    for half in range(2):
        out = refs[2 * SIDE + half]
        size = refs[0].shape[0]
        for index in range(SIDE):
            out[index * size : (index + 1) * size, :] = refs[SIDE * half + index][...]


def pack(first, second):
    size, width = first[0].shape
    shape = jax.ShapeDtypeStruct((SIDE * size, width), BF16)
    return pl.pallas_call(
        pack_body,
        out_shape=(shape, shape),
        in_specs=[whole()] * (2 * SIDE),
        out_specs=(whole(), whole()),
        compiler_params=params(),
        name="pack_ring",
    )(*first, *second)


def split_body(cut, *refs):
    for half in range(2):
        own, below, above = refs[3 * half : 3 * half + 3]
        outs = refs[6 + 5 * half : 11 + 5 * half]
        size = outs[0].shape[0]

        def total(index, cols):
            rows = slice(index * size, (index + 1) * size)
            return own[rows, cols] + below[rows, cols] + above[rows, cols]

        every = slice(None)
        outs[0][...] = total(0, every)
        outs[1][...] = total(1, every)
        outs[2][...] = total(2, slice(0, cut))
        outs[3][...] = total(2, slice(cut, None))
        outs[4][...] = total(3, every)


def split(first, second, cut):
    rows, width = first[0].shape
    shapes = piece_shapes(rows // SIDE, width, cut) * 2
    out = pl.pallas_call(
        functools.partial(split_body, cut),
        out_shape=tuple(shapes),
        in_specs=[whole()] * 6,
        out_specs=tuple([whole()] * 10),
        compiler_params=params(),
        name="split_ring",
    )(*first, *second)
    return out[:5], out[5:]


def route_body(experts, members, capacity, place_ref, ids_ref, other_ids_ref, w_ref, other_w_ref,
               pick_ref, extra_pick_ref, sent_ref, extra_sent_ref, weight_ref, extra_weight_ref, flag_ref):
    my_y, my_core, my_member = place_ref[0], place_ref[1], place_ref[2]
    tok_rows, top = ids_ref.shape
    tokens = 2 * tok_rows
    ids = jnp.concatenate([ids_ref[...], other_ids_ref[...]], axis=0)
    weights = jnp.concatenate([w_ref[...], other_w_ref[...]], axis=0).astype(F32)
    lane = lax.broadcasted_iota(jnp.int32, (tokens, experts), 1)
    group, member = div(lane, members), mod(lane, members)
    expert = (2 * group + my_core) * members + member
    named = jnp.zeros((tokens, experts), F32)
    weight = jnp.zeros((tokens, experts), F32)
    for k in range(top):
        hit = ids[:, k : k + 1] == expert
        named = jnp.where(hit, 1.0, named)
        weight = jnp.where(hit, weights[:, k : k + 1], weight)
    row = lax.broadcasted_iota(jnp.int32, (tokens, tokens), 0)
    col = lax.broadcasted_iota(jnp.int32, (tokens, tokens), 1)
    earlier = jnp.where(row > col, 1.0, 0.0).astype(BF16)
    before = dot(earlier, named.astype(BF16))

    counts = jnp.sum(named, axis=0, keepdims=True)
    lane1, group1 = lane[:1], group[:1]
    busiest = jnp.zeros((1, experts), jnp.bool_)
    for g in range(experts // members):
        inside = group1 == g
        most = jnp.max(jnp.where(inside, counts, -1.0), axis=1, keepdims=True)
        first = jnp.min(
            jnp.where(inside & (counts == most), lane1, experts), axis=1, keepdims=True
        )
        busiest = busiest | (lane1 == first)
    busy = jnp.where(busiest, 1.0, 0.0)
    lost = jnp.sum(jnp.where(before >= capacity, named * (1.0 - busy), 0.0), keepdims=True)
    mine = lane1 == my_y * members + my_member
    hot = jnp.sum(jnp.where(mine, busy, 0.0), axis=1, keepdims=True)
    flags = lax.broadcasted_iota(jnp.int32, (8, LANES), 1)
    flag_ref[...] = jnp.where(flags == 0, hot, jnp.where(flags == 1, jnp.minimum(lost, 1.0), 0.0))

    def places(total, expand, first_rank):
        slot = lax.broadcasted_iota(jnp.int32, (tokens, total), 1)
        want = (mod(slot, capacity) + first_rank).astype(F32)
        wide = lambda part: dot(part.astype(BF16), expand)
        taken = (wide(named_part) > 0.5) & (wide(before_part) == want)
        return taken, wide(weight_part)

    main = experts * capacity
    source = lax.broadcasted_iota(jnp.int32, (experts, main), 0)
    slot = lax.broadcasted_iota(jnp.int32, (experts, main), 1)
    named_part, before_part, weight_part = named, before, weight
    taken, value = places(
        main, jnp.where(div(slot, capacity) == source, 1.0, 0.0).astype(BF16), 0
    )
    picked = jnp.where(taken, 1.0, 0.0)
    pick_ref[...] = picked.astype(BF16)
    sent_ref[...] = picked.T.astype(BF16)
    weight_ref[...] = jnp.where(taken, value, 0.0).astype(BF16)

    extra = SIDE * capacity
    source = lax.broadcasted_iota(jnp.int32, (experts, extra), 0)
    slot = lax.broadcasted_iota(jnp.int32, (experts, extra), 1)
    target = div(slot, capacity) + my_y
    target = jnp.where(target >= SIDE, target - SIDE, target)
    named_part, before_part, weight_part = named * busy, before * busy, weight * busy
    taken, value = places(
        extra, jnp.where(div(source, members) == target, 1.0, 0.0).astype(BF16), capacity
    )
    picked = jnp.where(taken, 1.0, 0.0)
    extra_pick_ref[...] = picked.astype(BF16)
    extra_sent_ref[...] = picked.T.astype(BF16)
    extra_weight_ref[...] = jnp.where(taken, value, 0.0).astype(BF16)


def route(place, ids, other_ids, weights, other_weights, experts, members, capacity):
    tokens = 2 * ids.shape[0]
    main, extra = experts * capacity, SIDE * capacity
    return pl.pallas_call(
        functools.partial(route_body, experts, members, capacity),
        out_shape=(
            jax.ShapeDtypeStruct((tokens, main), BF16),
            jax.ShapeDtypeStruct((tokens, extra), BF16),
            jax.ShapeDtypeStruct((main, tokens), BF16),
            jax.ShapeDtypeStruct((extra, tokens), BF16),
            jax.ShapeDtypeStruct((tokens, main), BF16),
            jax.ShapeDtypeStruct((tokens, extra), BF16),
            jax.ShapeDtypeStruct((8, LANES), F32),
        ),
        in_specs=[pl.BlockSpec(memory_space=pltpu.SMEM)] + [whole()] * 4,
        out_specs=tuple([whole()] * 7),
        compiler_params=params(),
        name="route",
    )(place, ids, other_ids, weights, other_weights)


def dispatch_body(blocks, pick_ref, *refs):
    out_ref = refs[-1]
    half = refs[0].shape[0]
    for index in range(len(refs) // 2):
        own, other = refs[2 * index : 2 * index + 2]

        def fill(own=own, other=other):
            out_ref[...] = (
                dot(pick_ref[:, :half], own[...]) + dot(pick_ref[:, half:], other[...])
            ).astype(BF16)

        pl.when(div(pl.program_id(0), blocks) == index)(fill)


def dispatch(pick, pairs, block):
    tok_rows, width = pairs[0].shape
    slots = pick.shape[0]
    blocks = width // block
    arrays = len(pairs) // 2
    specs = []
    for index in range(arrays):
        columns = lambda i, index=index: (0, jnp.clip(i - index * blocks, 0, blocks - 1))
        specs += [pl.BlockSpec((tok_rows, block), columns)] * 2
    return pl.pallas_call(
        functools.partial(dispatch_body, blocks),
        out_shape=jax.ShapeDtypeStruct((slots, arrays * width), BF16),
        grid=(arrays * blocks,),
        in_specs=[pl.BlockSpec(pick.shape, lambda i: (0, 0))] + specs,
        out_specs=pl.BlockSpec((slots, block), lambda i: (0, i)),
        compiler_params=params(),
        cost_estimate=pl.CostEstimate(
            flops=4 * slots * tok_rows * width, bytes_accessed=4 * slots * width, transcendentals=0
        ),
        name="dispatch",
    )(pick, *pairs)


def slopes(gate, upper):
    sigma = jax.nn.sigmoid(gate)
    active = gate * sigma
    return upper * sigma * (1.0 + gate * (1.0 - sigma)), active, active * upper


def add_lanes(total_ref, here, product):
    partial = product[:, :LANES]
    for column in range(LANES, product.shape[1], LANES):
        partial = partial + product[:, column : column + LANES]
    total_ref[here, :] = jnp.where(pl.program_id(0) == 0, 0.0, total_ref[here, :]) + partial


def halves(total):
    return [slice(part * total // 2, (part + 1) * total // 2) for part in range(2)]


def extra_grads_body(cut, flag_ref, *refs):
    rows_refs, refs = refs[:10], refs[10:]
    gate_ref, up_ref, down_ref, d_gate_ref, d_up_ref, total_ref, rows = refs
    width = gate_ref.shape[0]
    keep = flag_ref[0:1, 0:1]

    @pl.when(pl.program_id(0) == 0)
    def _():
        put_pieces(rows, 0, rows_refs[:5], cut)
        put_pieces(rows, rows.shape[0] // 2, rows_refs[5:], cut)

    for here in halves(rows.shape[0]):
        slope, active, hidden = slopes(
            dot(rows[here, :width], gate_ref[...]), dot(rows[here, :width], up_ref[...])
        )
        raw = dot_t(rows[here, width:], down_ref[...]) * keep
        d_gate_ref[here, :] = (raw * slope).astype(BF16)
        d_up_ref[here, :] = (raw * active).astype(BF16)
        add_lanes(total_ref, here, raw * hidden)


def extra_grads(rows, flags, gate_mat, up_mat, down_mat, cut, block=256):
    width, hidden = gate_mat.shape
    total = rows[0].shape[0] * 2 * SIDE
    still = lambda i: (0, 0)
    return pl.pallas_call(
        functools.partial(extra_grads_body, cut),
        out_shape=(
            jax.ShapeDtypeStruct((total, hidden), BF16),
            jax.ShapeDtypeStruct((total, hidden), BF16),
            jax.ShapeDtypeStruct((total, LANES), F32),
        ),
        grid=(hidden // block,),
        in_specs=[pl.BlockSpec(flags.shape, still)]
        + [pl.BlockSpec(r.shape, still, pipeline_mode=pl.Buffered(1)) for r in rows]
        + [
            pl.BlockSpec((width, block), lambda i: (0, i)),
            pl.BlockSpec((width, block), lambda i: (0, i)),
            pl.BlockSpec((block, width), lambda i: (i, 0)),
        ],
        out_specs=(
            pl.BlockSpec((total, block), lambda i: (0, i)),
            pl.BlockSpec((total, block), lambda i: (0, i)),
            pl.BlockSpec((total, LANES), still),
        ),
        scratch_shapes=[pltpu.VMEM((total, 2 * width), BF16)],
        compiler_params=params(),
        cost_estimate=LITTLE,
        name="extra_grads",
    )(flags, *rows, gate_mat, up_mat, down_mat)


def forward_body(rows_ref, gate_ref, up_ref, slope_ref, active_ref, hidden_ref):
    for here in halves(rows_ref.shape[0]):
        rows = rows_ref[here, :]
        slope_ref[here, :], active_ref[here, :], hidden_ref[here, :] = slopes(
            dot(rows, gate_ref[...]), dot(rows, up_ref[...])
        )


def forward(rows, gate_mat, up_mat, block=256):
    width, hidden = gate_mat.shape
    total = rows.shape[0]
    state = jax.ShapeDtypeStruct((total, hidden), F32)
    columns = lambda i: (0, i)
    return pl.pallas_call(
        forward_body,
        out_shape=(state,) * 3,
        grid=(hidden // block,),
        in_specs=[
            pl.BlockSpec((total, width), lambda i: (0, 0), pipeline_mode=pl.Buffered(1)),
            pl.BlockSpec((width, block), columns),
            pl.BlockSpec((width, block), columns),
        ],
        out_specs=tuple([pl.BlockSpec((total, block), columns)] * 3),
        compiler_params=params(),
        cost_estimate=LITTLE,
        name="expert_forward",
    )(rows, gate_mat, up_mat)


def grads_body(rows_ref, down_ref, slope_ref, active_ref, hidden_ref, d_gate_ref, d_up_ref, total_ref):
    for here in halves(rows_ref.shape[0]):
        raw = dot_t(rows_ref[here, :], down_ref[...])
        d_gate_ref[here, :] = (raw * slope_ref[here, :]).astype(BF16)
        d_up_ref[here, :] = (raw * active_ref[here, :]).astype(BF16)
        add_lanes(total_ref, here, raw * hidden_ref[here, :])


def grads(rows, down_mat, slope, active, hidden_part, block=256):
    hidden, width = down_mat.shape
    total = rows.shape[0]
    columns = lambda i: (0, i)
    wide = pl.BlockSpec((total, block), columns)
    return pl.pallas_call(
        grads_body,
        out_shape=(
            jax.ShapeDtypeStruct((total, hidden), BF16),
            jax.ShapeDtypeStruct((total, hidden), BF16),
            jax.ShapeDtypeStruct((total, LANES), F32),
        ),
        grid=(hidden // block,),
        in_specs=[
            pl.BlockSpec((total, width), lambda i: (0, 0), pipeline_mode=pl.Buffered(1)),
            pl.BlockSpec((block, width), lambda i: (i, 0)),
            wide,
            wide,
            wide,
        ],
        out_specs=(wide, wide, pl.BlockSpec((total, LANES), lambda i: (0, 0))),
        compiler_params=params(),
        cost_estimate=pl.CostEstimate(
            flops=2 * total * width * hidden, bytes_accessed=24 << 20, transcendentals=0
        ),
        name="expert_grads",
    )(rows, down_mat, slope, active, hidden_part)


def contrib_body(cut, block, flag_ref, d_gate_ref, d_up_ref, total_ref, gate_ref, up_ref, *outs):
    step = pl.program_id(0)

    def tail(here):
        value = jnp.sum(total_ref[here, :], axis=1, keepdims=True)
        high = value.astype(BF16).astype(F32)
        lane = lax.broadcasted_iota(jnp.int32, (value.shape[0], LANES), 1)
        flag = jnp.where(lane == 2, flag_ref[0:1, 1:2], 0.0)
        return jnp.where(lane == 0, high, jnp.where(lane == 1, value - high, flag)).astype(BF16)

    result = (
        dot_t(d_gate_ref[...], gate_ref[...]) + dot_t(d_up_ref[...], up_ref[...])
    ).astype(BF16)
    if len(outs) == 1:
        columns = pl.ds(pl.multiple_of(step * block, block), block)
        outs[0][:, columns] = result

        @pl.when(step == 0)
        def _():
            outs[0][:, steps_width(outs[0]) :] = tail(slice(None))

        return
    size = outs[0].shape[0]
    low_steps = cut // block
    for half in range(2):
        own, below, far_low, far_high, above = outs[5 * half : 5 * half + 5]
        base = half * SIDE * size
        columns = pl.ds(pl.multiple_of(step * block, block), block)
        own[:, columns] = result[base : base + size]
        below[:, columns] = result[base + size : base + 2 * size]
        above[:, columns] = result[base + 3 * size : base + 4 * size]
        far = result[base + 2 * size : base + 3 * size]

        @pl.when(step < low_steps)
        def _():
            far_low[:, columns] = far

        @pl.when(step >= low_steps)
        def _():
            later = pl.multiple_of((step - low_steps) * block, block)
            far_high[:, pl.ds(later, block)] = far

        @pl.when(step == 0)
        def _():
            end = steps_width(own)
            own[:, end:] = tail(slice(base, base + size))
            below[:, end:] = tail(slice(base + size, base + 2 * size))
            above[:, end:] = tail(slice(base + 3 * size, base + 4 * size))
            far_high[:, end - cut :] = tail(slice(base + 2 * size, base + 3 * size))


def steps_width(ref):
    return ref.shape[1] - LANES


def contributions(flags, d_gate, d_up, total_part, gate_mat, up_mat, cut=None, block=512):
    total, hidden = d_gate.shape
    width = gate_mat.shape[0]
    if cut is None:
        shapes = [jax.ShapeDtypeStruct((total, width + LANES), BF16)]
    else:
        shapes = piece_shapes(total // (2 * SIDE), width + LANES, cut) * 2
    still = lambda i: (0, 0)
    out = pl.pallas_call(
        functools.partial(contrib_body, cut, block),
        out_shape=tuple(shapes),
        grid=(width // block,),
        in_specs=[
            pl.BlockSpec(flags.shape, still),
            pl.BlockSpec((total, hidden), still),
            pl.BlockSpec((total, hidden), still),
            pl.BlockSpec((total, LANES), still),
            pl.BlockSpec((block, hidden), lambda i: (i, 0)),
            pl.BlockSpec((block, hidden), lambda i: (i, 0)),
        ],
        out_specs=tuple(pl.BlockSpec(s.shape, still) for s in shapes),
        compiler_params=params(),
        cost_estimate=LITTLE
        if cut
        else pl.CostEstimate(
            flops=4 * total * width * hidden, bytes_accessed=40 << 20, transcendentals=0
        ),
        name="expert_contributions",
    )(flags, d_gate, d_up, total_part, gate_mat, up_mat)
    return out[0] if cut is None else (out[:5], out[5:])


def choices_body(members, capacity, place_ref, ids_ref, other_ids_ref, pick_ref, extra_pick_ref,
                 hit_ref, extra_hit_ref):
    my_y, my_core = place_ref[0], place_ref[1]
    ids = jnp.concatenate([ids_ref[...], other_ids_ref[...]], axis=0)
    tokens, top = ids.shape
    slot = div(lax.broadcasted_iota(jnp.int32, pick_ref.shape, 1), capacity)
    group, member = div(slot, members), mod(slot, members)
    expert = (2 * group + my_core) * members + member
    far_y = div(lax.broadcasted_iota(jnp.int32, extra_pick_ref.shape, 1), capacity) + my_y
    far_y = jnp.where(far_y >= SIDE, far_y - SIDE, far_y)
    far_group = 2 * far_y + my_core
    picked = pick_ref[...].astype(F32)
    extra_picked = extra_pick_ref[...].astype(F32)
    for k in range(top):
        here = slice(k * tokens, (k + 1) * tokens)
        name = ids[:, k : k + 1]
        hit = jnp.where(name == expert, picked, 0.0)
        placed = jnp.sum(hit, axis=1, keepdims=True)
        extra_hit = jnp.where(div(name, members) == far_group, extra_picked, 0.0)
        extra_hit = jnp.where(placed > 0.5, 0.0, extra_hit)
        hit_ref[here, :] = hit.astype(BF16)
        extra_hit_ref[here, :] = extra_hit.astype(BF16)


def choices(place, ids, other_ids, pick, extra_pick, members, capacity):
    top = ids.shape[1]
    return pl.pallas_call(
        functools.partial(choices_body, members, capacity),
        out_shape=(
            jax.ShapeDtypeStruct((top * pick.shape[0], pick.shape[1]), BF16),
            jax.ShapeDtypeStruct((top * pick.shape[0], extra_pick.shape[1]), BF16),
        ),
        in_specs=[pl.BlockSpec(memory_space=pltpu.SMEM)] + [whole()] * 4,
        out_specs=(whole(), whole()),
        compiler_params=params(),
        cost_estimate=LITTLE,
        name="choices",
    )(place, ids, other_ids, pick, extra_pick)


def combine_body(top, weight_ref, extra_weight_ref, hit_ref, extra_hit_ref, back_ref, extra_ref,
                 tail_ref, extra_tail_ref, sum_ref, other_sum_ref, route_ref, other_route_ref):
    total = dot(weight_ref[...], back_ref[...]) + dot(extra_weight_ref[...], extra_ref[...])
    half = sum_ref.shape[0]
    sum_ref[...] = total[:half]
    other_sum_ref[...] = total[half:]

    @pl.when(pl.program_id(0) == 0)
    def _():
        tail = tail_ref[...]
        value = dot(hit_ref[...], tail) + dot(extra_hit_ref[...], extra_tail_ref[...])
        tail_flags = tail.astype(F32)
        tail_lane = lax.broadcasted_iota(jnp.int32, tail_flags.shape, 1)
        flag = jnp.max(jnp.where(tail_lane == 2, tail_flags, 0.0), keepdims=True)
        lane = lax.broadcasted_iota(jnp.int32, (2 * half, LANES), 1)
        out = jnp.where(lane == top, flag, 0.0)
        for k in range(top):
            part = value[2 * half * k : 2 * half * (k + 1)]
            found = jnp.sum(jnp.where(lane < 2, part, 0.0), axis=1, keepdims=True)
            out = jnp.where(lane == k, found, out)
        route_ref[...] = out[:half]
        other_route_ref[...] = out[half:]


def combine(weight, extra_weight, hit, extra_hit, back, extra, block=1792):
    tokens, main = weight.shape
    rest = extra_weight.shape[1]
    width = back.shape[1] - LANES
    still = lambda i: (0, 0)
    columns = lambda i: (0, i)
    tail = lambda i: (0, width // LANES)
    sums = jax.ShapeDtypeStruct((tokens // 2, width), F32)
    routes = jax.ShapeDtypeStruct((tokens // 2, LANES), F32)
    return pl.pallas_call(
        functools.partial(combine_body, hit.shape[0] // tokens),
        out_shape=(sums, sums, routes, routes),
        grid=(width // block,),
        in_specs=[
            pl.BlockSpec(weight.shape, still),
            pl.BlockSpec(extra_weight.shape, still),
            pl.BlockSpec(hit.shape, still),
            pl.BlockSpec(extra_hit.shape, still),
            pl.BlockSpec((main, block), columns),
            pl.BlockSpec((rest, block), columns),
            pl.BlockSpec((main, LANES), tail),
            pl.BlockSpec((rest, LANES), tail),
        ],
        out_specs=tuple(
            [pl.BlockSpec((tokens // 2, block), columns)] * 2
            + [pl.BlockSpec(routes.shape, still)] * 2
        ),
        compiler_params=params(),
        name="combine",
    )(weight, extra_weight, hit, extra_hit, back, extra, back, extra)


def padded_path(tokens, out_grad, route_weights, expert_ids, gate_mat, up_mat, down_mat):
    tok_rows, width = tokens.shape
    top = expert_ids.shape[1]
    experts = lax.axis_size(ALL)
    capacity = 2 * tok_rows * top // experts
    named = jnp.any(expert_ids[:, :, None] == jnp.arange(experts, dtype=jnp.int32), axis=1)
    place = jnp.arange(tok_rows, dtype=jnp.int32)
    earlier = (place[:, None] > place[None, :]).astype(BF16)
    before = dot(earlier, named.astype(BF16)).astype(jnp.int32)
    slots = expert_ids * capacity + jnp.take_along_axis(before, expert_ids, axis=1)
    slot_iota = jnp.arange(experts * capacity, dtype=jnp.int32)
    taken = slots[:, :, None] == slot_iota[None, None, :]
    pick = jnp.any(taken, axis=1).astype(BF16)
    rows_x = exchange(dot_tl(pick, tokens).astype(BF16), ALL)
    rows_dy = exchange(dot_tl(pick, out_grad).astype(BF16), ALL)
    gate = dot(rows_x, gate_mat)
    upper = dot(rows_x, up_mat)
    sigma = jax.nn.sigmoid(gate)
    active = gate * sigma
    raw = dot_t(rows_dy, down_mat)
    routes = exchange(jnp.sum(raw * (active * upper), axis=1), ALL)
    d_gate = (raw * (upper * sigma * (1.0 + gate * (1.0 - sigma)))).astype(BF16)
    d_up = (raw * active).astype(BF16)
    back = exchange((dot_t(d_gate, gate_mat) + dot_t(d_up, up_mat)).astype(BF16), ALL)
    weights = jnp.sum(jnp.where(taken, route_weights[:, :, None], jnp.zeros((), BF16)), axis=1)
    x_grad = dot(weights, back).astype(BF16)
    return x_grad, jnp.sum(jnp.where(taken, routes[None, None, :], 0.0), axis=2)


def local(tokens, out_grad, route_weights, expert_ids, w_gate, w_up, w_down):
    tok_rows, width = tokens.shape
    top = expert_ids.shape[1]
    members = lax.axis_size("ingrp")
    experts = lax.axis_size(LIKE)
    capacity = tok_rows * top // experts
    main = experts * capacity
    mats = (w_gate[0], w_up[0], w_down[0])
    place = jnp.stack([lax.axis_index(name) for name in ALL]).astype(jnp.int32)

    other_ids, other_weights = swap(expert_ids), swap(route_weights)
    other_tokens, other_out_grad = swap(tokens), swap(out_grad)
    pick, extra_pick, sent_pick, extra_sent_pick, weight, extra_weight, flags = route(
        place, expert_ids, other_ids, route_weights, other_weights, experts, members, capacity
    )
    pair_x, pair_dy = (tokens, other_tokens), (out_grad, other_out_grad)

    cut, back_cut = width, 3 * 512
    extra = dispatch(extra_sent_pick, pair_x + pair_dy, 1792)
    parts = [extra[i * capacity : (i + 1) * capacity] for i in range(SIDE)]
    parts = parts[:1] + [shift_y(parts[i], i) for i in range(1, SIDE)]
    first = short_gather(jnp.concatenate(parts[:2], axis=0), 0)
    second = short_gather(jnp.concatenate(parts[2:], axis=0), 1)
    sent_x = dispatch(sent_pick, pair_x, 896)
    sent_x, first, second = lax.optimization_barrier((sent_x, first, second))
    rows_x = exchange(sent_x, LIKE)
    sent_dy = dispatch(sent_pick, pair_dy, 896)
    hit, extra_hit = choices(
        place, expert_ids, other_ids, pick, extra_pick, members, capacity
    )

    first, second = pack(first, second)
    first, second = near_gather(first, 1), near_gather(second, 0)
    rows_x, sent_dy, first, second = lax.optimization_barrier((rows_x, sent_dy, first, second))
    first, second = far_gather(first, 1, cut), far_gather(second, 0, cut)
    state = forward(rows_x, *mats[:2])
    sent_dy, state, first, second = lax.optimization_barrier((sent_dy, state, first, second))
    rows_dy = exchange(sent_dy, LIKE)

    first, second = contributions(
        flags, *extra_grads(first + second, flags, *mats, cut), *mats[:2], back_cut
    )
    first, second = fold_far((first, second), (1, 0), back_cut)
    rows_dy, first, second = lax.optimization_barrier((rows_dy, first, second))
    first, second = fold_near(first, 1), fold_near(second, 0)
    state = grads(rows_dy, mats[2], *state)
    first, second = split(first, second, back_cut)
    state, first, second = lax.optimization_barrier((state, first, second))
    first, second = fold_far((first, second), (0, 1), back_cut)
    result = contributions(flags, *state, *mats[:2])
    result, first, second = lax.optimization_barrier((result, first, second))
    back = exchange(result, LIKE)
    first, second = sum(fold_near(first, 0)), sum(fold_near(second, 1))
    parts = [first[:capacity], first[capacity:], second[:capacity], second[capacity:]]
    parts = parts[:1] + [shift_y(parts[i], -i) for i in range(1, SIDE)]
    extra_back = jnp.concatenate(parts, axis=0)

    sums, other_sums, routes, other_routes = combine(
        weight, extra_weight, hit, extra_hit, back, extra_back
    )
    x_grad = (sums + swap(other_sums)).astype(BF16)
    routes = routes + swap(other_routes)
    return lax.cond(
        routes[0, top] > 0,
        lambda: padded_path(tokens, out_grad, route_weights, expert_ids, *mats),
        lambda: (x_grad, routes[:, :top]),
    )


def solution(mesh):
    devices = mesh.devices
    split_mesh = Mesh(devices.reshape(devices.shape[0] // 2, 2, devices.shape[1]), ALL)
    rows = P(ALL, None)
    mats = P(ALL, None, None)
    return jax.shard_map(
        local,
        mesh=split_mesh,
        in_specs=(rows, rows, rows, rows, mats, mats, mats),
        out_specs=(rows, rows),
        check_vma=False,
    )
```

```python
import functools

import jax
import jax.numpy as jnp
from jax import lax
from jax.experimental import pallas as pl
from jax.experimental.pallas import tpu as pltpu
from jax.sharding import Mesh, PartitionSpec as P

ALL = ("y", "core", "ingrp")
LIKE = ("y", "ingrp")
SIDE = 4
LANES = 128
BF16 = jnp.bfloat16
F32 = jnp.float32
VMEM_LIMIT = 56 * 1024 * 1024
LITTLE = pl.CostEstimate(flops=1024, bytes_accessed=1024, transcendentals=0)


def params():
    return pltpu.CompilerParams(vmem_limit_bytes=VMEM_LIMIT)


def div(value, size):
    return lax.shift_right_logical(value, size.bit_length() - 1)


def mod(value, size):
    return value & (size - 1)


def whole():
    return pl.BlockSpec(memory_space=pltpu.VMEM)


def dot(left, right):
    return jnp.dot(left, right, preferred_element_type=F32)


def dot_t(left, right):
    return lax.dot_general(left, right, (((1,), (1,)), ((), ())), preferred_element_type=F32)


def dot_tl(left, right):
    return lax.dot_general(left, right, (((0,), (0,)), ((), ())), preferred_element_type=F32)


def exchange(rows, axes):
    count = lax.axis_size(axes)
    parts = rows.reshape((count, -1) + rows.shape[1:])
    return lax.all_to_all(parts, axes, split_axis=0, concat_axis=0, tiled=True).reshape(rows.shape)


def swap(rows):
    return lax.ppermute(rows, "core", [(0, 1), (1, 0)])


def shift(rows, axis, step):
    def target(index):
        place = [index // SIDE, index % SIDE]
        place[axis] = (place[axis] + step) % SIDE
        return place[0] * SIDE + place[1]

    return lax.ppermute(rows, "ingrp", [(i, target(i)) for i in range(SIDE * SIDE)])


def shift_y(rows, step):
    return lax.ppermute(rows, "y", [(i, (i + step) % SIDE) for i in range(SIDE)])


def short_gather(rows, axis):
    return rows, shift(rows, axis, 1), shift(rows, axis, 2), shift(rows, axis, -1)


def short_return(pieces, axis):
    own, below, far, above = pieces
    return own, shift(below, axis, -1), shift(far, axis, 2), shift(above, axis, 1)


def near_gather(rows, axis):
    return rows, shift(rows, axis, 1), shift(rows, axis, -1)


def far_gather(near, axis, cut):
    rows, below, above = near
    return [rows, below, shift(below[:, :cut], axis, 1), shift(above[:, cut:], axis, -1), above]


def fold_body(cut, *refs):
    for half in range(2):
        below, above, low, high = refs[4 * half : 4 * half + 4]
        out_below, out_above = refs[8 + 2 * half : 10 + 2 * half]
        out_below[:, :cut] = below[:, :cut] + low[...]
        out_below[:, cut:] = below[:, cut:]
        out_above[:, :cut] = above[:, :cut]
        out_above[:, cut:] = above[:, cut:] + high[...]


def fold_far(pieces, axes, cut):
    operands = []
    for (own, below, far_low, far_high, above), axis in zip(pieces, axes):
        operands += [below, above, shift(far_low, axis, -1), shift(far_high, axis, 1)]
    shape = jax.ShapeDtypeStruct(operands[0].shape, BF16)
    out = pl.pallas_call(
        functools.partial(fold_body, cut),
        out_shape=(shape,) * 4,
        in_specs=[whole()] * 8,
        out_specs=tuple([whole()] * 4),
        compiler_params=params(),
        name="fold_far",
    )(*operands)
    return (pieces[0][0], *out[:2]), (pieces[1][0], *out[2:])


def fold_near(pieces, axis):
    own, below, above = pieces
    return own, shift(below, axis, -1), shift(above, axis, 1)


def put_pieces(out, start, pieces, cut):
    size = pieces[0].shape[0]
    own, below, far_low, far_high, above = pieces
    out[start : start + size, :] = own[...]
    out[start + size : start + 2 * size, :] = below[...]
    out[start + 2 * size : start + 3 * size, :cut] = far_low[...]
    out[start + 2 * size : start + 3 * size, cut:] = far_high[...]
    out[start + 3 * size : start + 4 * size, :] = above[...]


def piece_shapes(size, width, cut):
    cols = [width, width, cut, width - cut, width]
    return [jax.ShapeDtypeStruct((size, c), BF16) for c in cols]


def pack_body(*refs):
    for half in range(2):
        out = refs[2 * SIDE + half]
        size = refs[0].shape[0]
        for index in range(SIDE):
            out[index * size : (index + 1) * size, :] = refs[SIDE * half + index][...]


def pack(first, second):
    size, width = first[0].shape
    shape = jax.ShapeDtypeStruct((SIDE * size, width), BF16)
    return pl.pallas_call(
        pack_body,
        out_shape=(shape, shape),
        in_specs=[whole()] * (2 * SIDE),
        out_specs=(whole(), whole()),
        compiler_params=params(),
        name="pack_ring",
    )(*first, *second)


def split_body(*refs):
    for half in range(2):
        own, below, above = refs[3 * half : 3 * half + 3]
        for index in range(SIDE):
            out = refs[6 + SIDE * half + index]
            size = out.shape[0]
            here = slice(index * size, (index + 1) * size)
            out[...] = own[here, :] + below[here, :] + above[here, :]


def split(first, second):
    rows, width = first[0].shape
    shape = jax.ShapeDtypeStruct((rows // SIDE, width), BF16)
    out = pl.pallas_call(
        split_body,
        out_shape=(shape,) * (2 * SIDE),
        in_specs=[whole()] * 6,
        out_specs=(whole(),) * (2 * SIDE),
        compiler_params=params(),
        name="split_ring",
    )(*first, *second)
    return out[:SIDE], out[SIDE:]


def route_body(experts, members, capacity, place_ref, ids_ref, other_ids_ref, w_ref, other_w_ref,
               pick_ref, extra_pick_ref, sent_ref, extra_sent_ref, weight_ref, extra_weight_ref, flag_ref):
    my_y, my_core, my_member = place_ref[0], place_ref[1], place_ref[2]
    tok_rows, top = ids_ref.shape
    tokens = 2 * tok_rows
    ids = jnp.concatenate([ids_ref[...], other_ids_ref[...]], axis=0)
    weights = jnp.concatenate([w_ref[...], other_w_ref[...]], axis=0).astype(F32)
    lane = lax.broadcasted_iota(jnp.int32, (tokens, experts), 1)
    group, member = div(lane, members), mod(lane, members)
    expert = (2 * group + my_core) * members + member
    named = jnp.zeros((tokens, experts), F32)
    weight = jnp.zeros((tokens, experts), F32)
    for k in range(top):
        hit = ids[:, k : k + 1] == expert
        named = jnp.where(hit, 1.0, named)
        weight = jnp.where(hit, weights[:, k : k + 1], weight)
    row = lax.broadcasted_iota(jnp.int32, (tokens, tokens), 0)
    col = lax.broadcasted_iota(jnp.int32, (tokens, tokens), 1)
    earlier = jnp.where(row > col, 1.0, 0.0).astype(BF16)
    before = dot(earlier, named.astype(BF16))

    counts = jnp.sum(named, axis=0, keepdims=True)
    lane1, group1 = lane[:1], group[:1]
    busiest = jnp.zeros((1, experts), jnp.bool_)
    for g in range(experts // members):
        inside = group1 == g
        most = jnp.max(jnp.where(inside, counts, -1.0), axis=1, keepdims=True)
        first = jnp.min(
            jnp.where(inside & (counts == most), lane1, experts), axis=1, keepdims=True
        )
        busiest = busiest | (lane1 == first)
    busy = jnp.where(busiest, 1.0, 0.0)
    lost = jnp.sum(jnp.where(before >= capacity, named * (1.0 - busy), 0.0), keepdims=True)
    mine = lane1 == my_y * members + my_member
    hot = jnp.sum(jnp.where(mine, busy, 0.0), axis=1, keepdims=True)
    flags = lax.broadcasted_iota(jnp.int32, (8, LANES), 1)
    flag_ref[...] = jnp.where(flags == 0, hot, jnp.where(flags == 1, jnp.minimum(lost, 1.0), 0.0))

    def places(total, expand, first_rank):
        slot = lax.broadcasted_iota(jnp.int32, (tokens, total), 1)
        want = (mod(slot, capacity) + first_rank).astype(F32)
        wide = lambda part: dot(part.astype(BF16), expand)
        taken = (wide(named_part) > 0.5) & (wide(before_part) == want)
        return taken, wide(weight_part)

    main = experts * capacity
    source = lax.broadcasted_iota(jnp.int32, (experts, main), 0)
    slot = lax.broadcasted_iota(jnp.int32, (experts, main), 1)
    named_part, before_part, weight_part = named, before, weight
    taken, value = places(
        main, jnp.where(div(slot, capacity) == source, 1.0, 0.0).astype(BF16), 0
    )
    picked = jnp.where(taken, 1.0, 0.0)
    pick_ref[...] = picked.astype(BF16)
    sent_ref[...] = picked.T.astype(BF16)
    weight_ref[...] = jnp.where(taken, value, 0.0).astype(BF16)

    extra = SIDE * capacity
    source = lax.broadcasted_iota(jnp.int32, (experts, extra), 0)
    slot = lax.broadcasted_iota(jnp.int32, (experts, extra), 1)
    target = div(slot, capacity) + my_y
    target = jnp.where(target >= SIDE, target - SIDE, target)
    named_part, before_part, weight_part = named * busy, before * busy, weight * busy
    taken, value = places(
        extra, jnp.where(div(source, members) == target, 1.0, 0.0).astype(BF16), capacity
    )
    picked = jnp.where(taken, 1.0, 0.0)
    extra_pick_ref[...] = picked.astype(BF16)
    extra_sent_ref[...] = picked.T.astype(BF16)
    extra_weight_ref[...] = jnp.where(taken, value, 0.0).astype(BF16)


def route(place, ids, other_ids, weights, other_weights, experts, members, capacity):
    tokens = 2 * ids.shape[0]
    main, extra = experts * capacity, SIDE * capacity
    return pl.pallas_call(
        functools.partial(route_body, experts, members, capacity),
        out_shape=(
            jax.ShapeDtypeStruct((tokens, main), BF16),
            jax.ShapeDtypeStruct((tokens, extra), BF16),
            jax.ShapeDtypeStruct((main, tokens), BF16),
            jax.ShapeDtypeStruct((extra, tokens), BF16),
            jax.ShapeDtypeStruct((tokens, main), BF16),
            jax.ShapeDtypeStruct((tokens, extra), BF16),
            jax.ShapeDtypeStruct((8, LANES), F32),
        ),
        in_specs=[pl.BlockSpec(memory_space=pltpu.SMEM)] + [whole()] * 4,
        out_specs=tuple([whole()] * 7),
        compiler_params=params(),
        name="route",
    )(place, ids, other_ids, weights, other_weights)


def dispatch_body(blocks, pick_ref, *refs):
    out_ref = refs[-1]
    half = refs[0].shape[0]
    for index in range(len(refs) // 2):
        own, other = refs[2 * index : 2 * index + 2]

        def fill(own=own, other=other):
            out_ref[...] = (
                dot(pick_ref[:, :half], own[...]) + dot(pick_ref[:, half:], other[...])
            ).astype(BF16)

        pl.when(div(pl.program_id(0), blocks) == index)(fill)


def dispatch(pick, pairs, block):
    tok_rows, width = pairs[0].shape
    slots = pick.shape[0]
    blocks = width // block
    arrays = len(pairs) // 2
    specs = []
    for index in range(arrays):
        columns = lambda i, index=index: (0, jnp.clip(i - index * blocks, 0, blocks - 1))
        specs += [pl.BlockSpec((tok_rows, block), columns)] * 2
    return pl.pallas_call(
        functools.partial(dispatch_body, blocks),
        out_shape=jax.ShapeDtypeStruct((slots, arrays * width), BF16),
        grid=(arrays * blocks,),
        in_specs=[pl.BlockSpec(pick.shape, lambda i: (0, 0))] + specs,
        out_specs=pl.BlockSpec((slots, block), lambda i: (0, i)),
        compiler_params=params(),
        cost_estimate=pl.CostEstimate(
            flops=4 * slots * tok_rows * width, bytes_accessed=4 * slots * width, transcendentals=0
        ),
        name="dispatch",
    )(pick, *pairs)


def slopes(gate, upper):
    sigma = jax.nn.sigmoid(gate)
    active = gate * sigma
    return upper * sigma * (1.0 + gate * (1.0 - sigma)), active, active * upper


def add_lanes(total_ref, here, product):
    partial = product[:, :LANES]
    for column in range(LANES, product.shape[1], LANES):
        partial = partial + product[:, column : column + LANES]
    total_ref[here, :] = jnp.where(pl.program_id(0) == 0, 0.0, total_ref[here, :]) + partial


def halves(total):
    return [slice(part * total // 2, (part + 1) * total // 2) for part in range(2)]


def extra_grads_body(cut, flag_ref, *refs):
    rows_refs, refs = refs[:10], refs[10:]
    gate_ref, up_ref, down_ref, d_gate_ref, d_up_ref, total_ref, rows = refs
    width = gate_ref.shape[0]
    keep = flag_ref[0:1, 0:1]

    @pl.when(pl.program_id(0) == 0)
    def _():
        put_pieces(rows, 0, rows_refs[:5], cut)
        put_pieces(rows, rows.shape[0] // 2, rows_refs[5:], cut)

    for here in halves(rows.shape[0]):
        slope, active, hidden = slopes(
            dot(rows[here, :width], gate_ref[...]), dot(rows[here, :width], up_ref[...])
        )
        raw = dot_t(rows[here, width:], down_ref[...]) * keep
        d_gate_ref[here, :] = (raw * slope).astype(BF16)
        d_up_ref[here, :] = (raw * active).astype(BF16)
        add_lanes(total_ref, here, raw * hidden)


def extra_grads(rows, flags, gate_mat, up_mat, down_mat, cut, block=256):
    width, hidden = gate_mat.shape
    total = rows[0].shape[0] * 2 * SIDE
    still = lambda i: (0, 0)
    return pl.pallas_call(
        functools.partial(extra_grads_body, cut),
        out_shape=(
            jax.ShapeDtypeStruct((total, hidden), BF16),
            jax.ShapeDtypeStruct((total, hidden), BF16),
            jax.ShapeDtypeStruct((total, LANES), F32),
        ),
        grid=(hidden // block,),
        in_specs=[pl.BlockSpec(flags.shape, still)]
        + [pl.BlockSpec(r.shape, still, pipeline_mode=pl.Buffered(1)) for r in rows]
        + [
            pl.BlockSpec((width, block), lambda i: (0, i)),
            pl.BlockSpec((width, block), lambda i: (0, i)),
            pl.BlockSpec((block, width), lambda i: (i, 0)),
        ],
        out_specs=(
            pl.BlockSpec((total, block), lambda i: (0, i)),
            pl.BlockSpec((total, block), lambda i: (0, i)),
            pl.BlockSpec((total, LANES), still),
        ),
        scratch_shapes=[pltpu.VMEM((total, 2 * width), BF16)],
        compiler_params=params(),
        cost_estimate=LITTLE,
        name="extra_grads",
    )(flags, *rows, gate_mat, up_mat, down_mat)


def forward_body(rows_ref, gate_ref, up_ref, slope_ref, active_ref, hidden_ref):
    for here in halves(rows_ref.shape[0]):
        rows = rows_ref[here, :]
        slope_ref[here, :], active_ref[here, :], hidden_ref[here, :] = slopes(
            dot(rows, gate_ref[...]), dot(rows, up_ref[...])
        )


def forward(rows, gate_mat, up_mat, block=256):
    width, hidden = gate_mat.shape
    total = rows.shape[0]
    state = jax.ShapeDtypeStruct((total, hidden), F32)
    columns = lambda i: (0, i)
    return pl.pallas_call(
        forward_body,
        out_shape=(state,) * 3,
        grid=(hidden // block,),
        in_specs=[
            pl.BlockSpec((total, width), lambda i: (0, 0), pipeline_mode=pl.Buffered(1)),
            pl.BlockSpec((width, block), columns),
            pl.BlockSpec((width, block), columns),
        ],
        out_specs=tuple([pl.BlockSpec((total, block), columns)] * 3),
        compiler_params=params(),
        cost_estimate=LITTLE,
        name="expert_forward",
    )(rows, gate_mat, up_mat)


def grads_body(rows_ref, down_ref, slope_ref, active_ref, hidden_ref, d_gate_ref, d_up_ref, total_ref):
    for here in halves(rows_ref.shape[0]):
        raw = dot_t(rows_ref[here, :], down_ref[...])
        d_gate_ref[here, :] = (raw * slope_ref[here, :]).astype(BF16)
        d_up_ref[here, :] = (raw * active_ref[here, :]).astype(BF16)
        add_lanes(total_ref, here, raw * hidden_ref[here, :])


def grads(rows, down_mat, slope, active, hidden_part, block=256):
    hidden, width = down_mat.shape
    total = rows.shape[0]
    columns = lambda i: (0, i)
    wide = pl.BlockSpec((total, block), columns)
    return pl.pallas_call(
        grads_body,
        out_shape=(
            jax.ShapeDtypeStruct((total, hidden), BF16),
            jax.ShapeDtypeStruct((total, hidden), BF16),
            jax.ShapeDtypeStruct((total, LANES), F32),
        ),
        grid=(hidden // block,),
        in_specs=[
            pl.BlockSpec((total, width), lambda i: (0, 0), pipeline_mode=pl.Buffered(1)),
            pl.BlockSpec((block, width), lambda i: (i, 0)),
            wide,
            wide,
            wide,
        ],
        out_specs=(wide, wide, pl.BlockSpec((total, LANES), lambda i: (0, 0))),
        compiler_params=params(),
        cost_estimate=pl.CostEstimate(
            flops=2 * total * width * hidden, bytes_accessed=24 << 20, transcendentals=0
        ),
        name="expert_grads",
    )(rows, down_mat, slope, active, hidden_part)


def contrib_body(cut, block, flag_ref, d_gate_ref, d_up_ref, total_ref, gate_ref, up_ref, *outs):
    step = pl.program_id(0)

    def tail(here):
        value = jnp.sum(total_ref[here, :], axis=1, keepdims=True)
        high = value.astype(BF16).astype(F32)
        lane = lax.broadcasted_iota(jnp.int32, (value.shape[0], LANES), 1)
        flag = jnp.where(lane == 2, flag_ref[0:1, 1:2], 0.0)
        return jnp.where(lane == 0, high, jnp.where(lane == 1, value - high, flag)).astype(BF16)

    result = (
        dot_t(d_gate_ref[...], gate_ref[...]) + dot_t(d_up_ref[...], up_ref[...])
    ).astype(BF16)
    if len(outs) == 1:
        columns = pl.ds(pl.multiple_of(step * block, block), block)
        outs[0][:, columns] = result

        @pl.when(step == 0)
        def _():
            outs[0][:, steps_width(outs[0]) :] = tail(slice(None))

        return
    size = outs[0].shape[0]
    low_steps = cut // block
    for half in range(2):
        own, below, far_low, far_high, above = outs[5 * half : 5 * half + 5]
        base = half * SIDE * size
        columns = pl.ds(pl.multiple_of(step * block, block), block)
        own[:, columns] = result[base : base + size]
        below[:, columns] = result[base + size : base + 2 * size]
        above[:, columns] = result[base + 3 * size : base + 4 * size]
        far = result[base + 2 * size : base + 3 * size]

        @pl.when(step < low_steps)
        def _():
            far_low[:, columns] = far

        @pl.when(step >= low_steps)
        def _():
            later = pl.multiple_of((step - low_steps) * block, block)
            far_high[:, pl.ds(later, block)] = far

        @pl.when(step == 0)
        def _():
            end = steps_width(own)
            own[:, end:] = tail(slice(base, base + size))
            below[:, end:] = tail(slice(base + size, base + 2 * size))
            above[:, end:] = tail(slice(base + 3 * size, base + 4 * size))
            far_high[:, end - cut :] = tail(slice(base + 2 * size, base + 3 * size))


def steps_width(ref):
    return ref.shape[1] - LANES


def contributions(flags, d_gate, d_up, total_part, gate_mat, up_mat, cut=None, block=512):
    total, hidden = d_gate.shape
    width = gate_mat.shape[0]
    if cut is None:
        shapes = [jax.ShapeDtypeStruct((total, width + LANES), BF16)]
    else:
        shapes = piece_shapes(total // (2 * SIDE), width + LANES, cut) * 2
    still = lambda i: (0, 0)
    out = pl.pallas_call(
        functools.partial(contrib_body, cut, block),
        out_shape=tuple(shapes),
        grid=(width // block,),
        in_specs=[
            pl.BlockSpec(flags.shape, still),
            pl.BlockSpec((total, hidden), still),
            pl.BlockSpec((total, hidden), still),
            pl.BlockSpec((total, LANES), still),
            pl.BlockSpec((block, hidden), lambda i: (i, 0)),
            pl.BlockSpec((block, hidden), lambda i: (i, 0)),
        ],
        out_specs=tuple(pl.BlockSpec(s.shape, still) for s in shapes),
        compiler_params=params(),
        cost_estimate=LITTLE
        if cut
        else pl.CostEstimate(
            flops=4 * total * width * hidden, bytes_accessed=40 << 20, transcendentals=0
        ),
        name="expert_contributions",
    )(flags, d_gate, d_up, total_part, gate_mat, up_mat)
    return out[0] if cut is None else (out[:5], out[5:])


def choices_body(members, capacity, place_ref, ids_ref, other_ids_ref, pick_ref, extra_pick_ref,
                 *outs):
    my_y, my_core = place_ref[0], place_ref[1]
    ids = jnp.concatenate([ids_ref[...], other_ids_ref[...]], axis=0)
    tokens, top = ids.shape
    slot = div(lax.broadcasted_iota(jnp.int32, pick_ref.shape, 1), capacity)
    group, member = div(slot, members), mod(slot, members)
    expert = (2 * group + my_core) * members + member
    far_y = div(lax.broadcasted_iota(jnp.int32, extra_pick_ref.shape, 1), capacity) + my_y
    far_y = jnp.where(far_y >= SIDE, far_y - SIDE, far_y)
    far_group = 2 * far_y + my_core
    picked = pick_ref[...].astype(F32)
    extra_picked = extra_pick_ref[...].astype(F32)
    half = tokens // 2
    for k in range(top):
        here = slice(k * half, (k + 1) * half)
        name = ids[:, k : k + 1]
        hit = jnp.where(name == expert, picked, 0.0)
        placed = jnp.sum(hit, axis=1, keepdims=True)
        extra_hit = jnp.where(div(name, members) == far_group, extra_picked, 0.0)
        extra_hit = jnp.where(placed > 0.5, 0.0, extra_hit)
        outs[0][here, :] = hit[:half].astype(BF16)
        outs[1][here, :] = extra_hit[:half].astype(BF16)
        outs[2][here, :] = hit[half:].astype(BF16)
        outs[3][here, :] = extra_hit[half:].astype(BF16)


def choices(place, ids, other_ids, pick, extra_pick, members, capacity):
    rows = ids.shape[0] * ids.shape[1]
    shapes = [jax.ShapeDtypeStruct((rows, p.shape[1]), BF16) for p in (pick, extra_pick)]
    return pl.pallas_call(
        functools.partial(choices_body, members, capacity),
        out_shape=tuple(shapes * 2),
        in_specs=[pl.BlockSpec(memory_space=pltpu.SMEM)] + [whole()] * 4,
        out_specs=(whole(),) * 4,
        compiler_params=params(),
        cost_estimate=LITTLE,
        name="choices",
    )(place, ids, other_ids, pick, extra_pick)


def choice_sums(top, tokens, hit_ref, extra_hit_ref, tail_ref, extra_tail_ref):
    tail = tail_ref[...]
    value = dot(hit_ref[...], tail) + dot(extra_hit_ref[...], extra_tail_ref[...])
    flags = tail.astype(F32)
    flag_lane = lax.broadcasted_iota(jnp.int32, flags.shape, 1)
    flag = jnp.max(jnp.where(flag_lane == 2, flags, 0.0), keepdims=True)
    lane = lax.broadcasted_iota(jnp.int32, (tokens, LANES), 1)
    out = jnp.where(lane == top, flag, 0.0)
    for k in range(top):
        part = value[tokens * k : tokens * (k + 1)]
        found = jnp.sum(jnp.where(lane < 2, part, 0.0), axis=1, keepdims=True)
        out = jnp.where(lane == k, found, out)
    return out


def combine_specs(half, weight, extra_weight, hit, extra_hit, width, block, columns):
    still = lambda *_: (0, 0)
    mine = lambda *_: (half, 0)
    tail = lambda *_: (0, width // LANES)
    tokens, main = weight.shape[0] // 2, weight.shape[1]
    rest = extra_weight.shape[1]
    return [
        pl.BlockSpec((tokens, main), mine),
        pl.BlockSpec((tokens, rest), mine),
        pl.BlockSpec(hit.shape, still),
        pl.BlockSpec(extra_hit.shape, still),
        pl.BlockSpec((main, block), columns),
        pl.BlockSpec((rest, block), columns),
        pl.BlockSpec((main, LANES), tail),
        pl.BlockSpec((rest, LANES), tail),
    ]


def send_body(top, weight_ref, extra_weight_ref, hit_ref, extra_hit_ref, back_ref, extra_ref,
              tail_ref, extra_tail_ref, sum_ref, route_ref):
    sum_ref[...] = dot(weight_ref[...], back_ref[...]) + dot(extra_weight_ref[...], extra_ref[...])

    @pl.when(pl.program_id(0) == 0)
    def _():
        route_ref[...] = choice_sums(
            top, sum_ref.shape[0], hit_ref, extra_hit_ref, tail_ref, extra_tail_ref
        )


def combine_other(weight, extra_weight, hit, extra_hit, back, extra, block=1792):
    tokens = weight.shape[0] // 2
    width = back.shape[1] - LANES
    columns = lambda i: (0, i)
    return pl.pallas_call(
        functools.partial(send_body, hit.shape[0] // tokens),
        out_shape=(
            jax.ShapeDtypeStruct((tokens, width), F32),
            jax.ShapeDtypeStruct((tokens, LANES), F32),
        ),
        grid=(width // block,),
        in_specs=combine_specs(1, weight, extra_weight, hit, extra_hit, width, block, columns),
        out_specs=(
            pl.BlockSpec((tokens, block), columns),
            pl.BlockSpec((tokens, LANES), lambda i: (0, 0)),
        ),
        compiler_params=params(),
        name="combine_other",
    )(weight, extra_weight, hit, extra_hit, back, extra, back, extra)


def combine_body(top, weight_ref, extra_weight_ref, hit_ref, extra_hit_ref, back_ref, extra_ref,
                 tail_ref, extra_tail_ref, other_ref, other_route_ref, x_grad_ref, route_ref):
    total = dot(weight_ref[...], back_ref[...]) + dot(extra_weight_ref[...], extra_ref[...])
    x_grad_ref[...] = (total + other_ref[...]).astype(BF16)

    @pl.when(pl.program_id(0) == 0)
    def _():
        route_ref[...] = other_route_ref[...] + choice_sums(
            top, total.shape[0], hit_ref, extra_hit_ref, tail_ref, extra_tail_ref
        )


def combine(weight, extra_weight, hit, extra_hit, back, extra, other_sums, other_routes, block=1792):
    tokens, width = other_sums.shape
    columns = lambda i: (0, i)
    still = lambda i: (0, 0)
    wide = pl.BlockSpec((tokens, block), columns)
    narrow = pl.BlockSpec((tokens, LANES), still)
    return pl.pallas_call(
        functools.partial(combine_body, hit.shape[0] // tokens),
        out_shape=(
            jax.ShapeDtypeStruct((tokens, width), BF16),
            jax.ShapeDtypeStruct((tokens, LANES), F32),
        ),
        grid=(width // block,),
        in_specs=combine_specs(0, weight, extra_weight, hit, extra_hit, width, block, columns)
        + [wide, narrow],
        out_specs=(wide, narrow),
        compiler_params=params(),
        name="combine",
    )(weight, extra_weight, hit, extra_hit, back, extra, back, extra, other_sums, other_routes)


def padded_path(tokens, out_grad, route_weights, expert_ids, gate_mat, up_mat, down_mat):
    tok_rows, width = tokens.shape
    top = expert_ids.shape[1]
    experts = lax.axis_size(ALL)
    capacity = 2 * tok_rows * top // experts
    named = jnp.any(expert_ids[:, :, None] == jnp.arange(experts, dtype=jnp.int32), axis=1)
    place = jnp.arange(tok_rows, dtype=jnp.int32)
    earlier = (place[:, None] > place[None, :]).astype(BF16)
    before = dot(earlier, named.astype(BF16)).astype(jnp.int32)
    slots = expert_ids * capacity + jnp.take_along_axis(before, expert_ids, axis=1)
    slot_iota = jnp.arange(experts * capacity, dtype=jnp.int32)
    taken = slots[:, :, None] == slot_iota[None, None, :]
    pick = jnp.any(taken, axis=1).astype(BF16)
    rows_x = exchange(dot_tl(pick, tokens).astype(BF16), ALL)
    rows_dy = exchange(dot_tl(pick, out_grad).astype(BF16), ALL)
    gate = dot(rows_x, gate_mat)
    upper = dot(rows_x, up_mat)
    sigma = jax.nn.sigmoid(gate)
    active = gate * sigma
    raw = dot_t(rows_dy, down_mat)
    routes = exchange(jnp.sum(raw * (active * upper), axis=1), ALL)
    d_gate = (raw * (upper * sigma * (1.0 + gate * (1.0 - sigma)))).astype(BF16)
    d_up = (raw * active).astype(BF16)
    back = exchange((dot_t(d_gate, gate_mat) + dot_t(d_up, up_mat)).astype(BF16), ALL)
    weights = jnp.sum(jnp.where(taken, route_weights[:, :, None], jnp.zeros((), BF16)), axis=1)
    x_grad = dot(weights, back).astype(BF16)
    return x_grad, jnp.sum(jnp.where(taken, routes[None, None, :], 0.0), axis=2)


def local(tokens, out_grad, route_weights, expert_ids, w_gate, w_up, w_down):
    tok_rows, width = tokens.shape
    top = expert_ids.shape[1]
    members = lax.axis_size("ingrp")
    experts = lax.axis_size(LIKE)
    capacity = tok_rows * top // experts
    main = experts * capacity
    mats = (w_gate[0], w_up[0], w_down[0])
    place = jnp.stack([lax.axis_index(name) for name in ALL]).astype(jnp.int32)

    other_ids, other_weights = swap(expert_ids), swap(route_weights)
    other_tokens, other_out_grad = swap(tokens), swap(out_grad)
    pick, extra_pick, sent_pick, extra_sent_pick, weight, extra_weight, flags = route(
        place, expert_ids, other_ids, route_weights, other_weights, experts, members, capacity
    )
    pair_x, pair_dy = (tokens, other_tokens), (out_grad, other_out_grad)

    cut, back_cut = width, 3 * 512
    extra = dispatch(extra_sent_pick, pair_x + pair_dy, 3584)
    parts = [extra[i * capacity : (i + 1) * capacity] for i in range(SIDE)]
    parts = parts[:1] + [shift_y(parts[i], i) for i in range(1, SIDE)]
    sent_x = dispatch(sent_pick, pair_x, 896)
    sent_x, *parts = lax.optimization_barrier((sent_x, *parts))
    first = short_gather(jnp.concatenate(parts[:2], axis=0), 0)
    second = short_gather(jnp.concatenate(parts[2:], axis=0), 1)
    sent_x, first, second = lax.optimization_barrier((sent_x, first, second))
    rows_x = exchange(sent_x, LIKE)

    first, second = pack(first, second)
    sent_dy = dispatch(sent_pick, pair_dy, 896)
    hits = choices(place, expert_ids, other_ids, pick, extra_pick, members, capacity)
    first, second, sent_dy, hits = lax.optimization_barrier((first, second, sent_dy, hits))
    first, second = near_gather(first, 1), near_gather(second, 0)
    state = forward(rows_x, *mats[:2])
    state, sent_dy, first, second = lax.optimization_barrier((state, sent_dy, first, second))
    first, second = far_gather(first, 1, cut), far_gather(second, 0, cut)
    sent_dy, first, second = lax.optimization_barrier((sent_dy, first, second))
    rows_dy = exchange(sent_dy, LIKE)

    first, second = contributions(
        flags, *extra_grads(first + second, flags, *mats, cut), *mats[:2], back_cut
    )
    first, second = fold_far((first, second), (1, 0), back_cut)
    rows_dy, first, second = lax.optimization_barrier((rows_dy, first, second))
    first, second = fold_near(first, 1), fold_near(second, 0)
    state = grads(rows_dy, mats[2], *state)
    first, second = split(first, second)
    state, first, second = lax.optimization_barrier((state, first, second))
    first, second = short_return(first, 0), short_return(second, 1)
    result = contributions(flags, *state, *mats[:2])
    result, first, second = lax.optimization_barrier((result, first, second))
    back = exchange(result, LIKE)
    first, second = sum(first[1:], first[0]), sum(second[1:], second[0])
    parts = [first[:capacity], first[capacity:], second[:capacity], second[capacity:]]
    parts = parts[:1] + [shift_y(parts[i], -i) for i in range(1, SIDE)]
    extra_back = jnp.concatenate(parts, axis=0)

    weights = (weight, extra_weight)
    other_sums, other_routes = combine_other(*weights, *hits[2:], back, extra_back)
    x_grad, routes = combine(
        *weights, *hits[:2], back, extra_back, swap(other_sums), swap(other_routes)
    )
    return lax.cond(
        routes[0, top] > 0,
        lambda: padded_path(tokens, out_grad, route_weights, expert_ids, *mats),
        lambda: (x_grad, routes[:, :top]),
    )


def solution(mesh):
    devices = mesh.devices
    split_mesh = Mesh(devices.reshape(devices.shape[0] // 2, 2, devices.shape[1]), ALL)
    rows = P(ALL, None)
    mats = P(ALL, None, None)
    return jax.shard_map(
        local,
        mesh=split_mesh,
        in_specs=(rows, rows, rows, rows, mats, mats, mats),
        out_specs=(rows, rows),
        check_vma=False,
    )
```

```python
import functools

import jax
import jax.numpy as jnp
from jax import lax
from jax.experimental import pallas as pl
from jax.experimental.pallas import tpu as pltpu
from jax.sharding import Mesh, PartitionSpec as P

ALL = ("y", "core", "ingrp")
LIKE = ("y", "ingrp")
SIDE = 4
LANES = 128
BF16 = jnp.bfloat16
F32 = jnp.float32
VMEM_LIMIT = 56 * 1024 * 1024
LITTLE = pl.CostEstimate(flops=1024, bytes_accessed=1024, transcendentals=0)


def params():
    return pltpu.CompilerParams(vmem_limit_bytes=VMEM_LIMIT)


def div(value, size):
    return lax.shift_right_logical(value, size.bit_length() - 1)


def mod(value, size):
    return value & (size - 1)


def whole():
    return pl.BlockSpec(memory_space=pltpu.VMEM)


def dot(left, right):
    return jnp.dot(left, right, preferred_element_type=F32)


def dot_t(left, right):
    return lax.dot_general(left, right, (((1,), (1,)), ((), ())), preferred_element_type=F32)


def dot_tl(left, right):
    return lax.dot_general(left, right, (((0,), (0,)), ((), ())), preferred_element_type=F32)


def exchange(rows, axes):
    count = lax.axis_size(axes)
    parts = rows.reshape((count, -1) + rows.shape[1:])
    return lax.all_to_all(parts, axes, split_axis=0, concat_axis=0, tiled=True).reshape(rows.shape)


def swap(rows):
    return lax.ppermute(rows, "core", [(0, 1), (1, 0)])


def shift(rows, axis, step):
    def target(index):
        place = [index // SIDE, index % SIDE]
        place[axis] = (place[axis] + step) % SIDE
        return place[0] * SIDE + place[1]

    return lax.ppermute(rows, "ingrp", [(i, target(i)) for i in range(SIDE * SIDE)])


def shift_y(rows, step):
    return lax.ppermute(rows, "y", [(i, (i + step) % SIDE) for i in range(SIDE)])


def short_gather(rows, axis):
    return rows, shift(rows, axis, 1), shift(rows, axis, 2), shift(rows, axis, -1)


def short_return(pieces, axis):
    own, below, far, above = pieces
    return own, shift(below, axis, -1), shift(far, axis, 2), shift(above, axis, 1)


def near_gather(rows, axis):
    return rows, shift(rows, axis, 1), shift(rows, axis, -1)


def far_gather(near, axis, cut):
    rows, below, above = near
    return [rows, below, shift(below[:, :cut], axis, 1), shift(above[:, cut:], axis, -1), above]


def fold_body(cut, *refs):
    for half in range(2):
        below, above, low, high = refs[4 * half : 4 * half + 4]
        out_below, out_above = refs[8 + 2 * half : 10 + 2 * half]
        out_below[:, :cut] = below[:, :cut] + low[...]
        out_below[:, cut:] = below[:, cut:]
        out_above[:, :cut] = above[:, :cut]
        out_above[:, cut:] = above[:, cut:] + high[...]


def fold_far(pieces, axes, cut):
    operands = []
    for (own, below, far_low, far_high, above), axis in zip(pieces, axes):
        operands += [below, above, shift(far_low, axis, -1), shift(far_high, axis, 1)]
    shape = jax.ShapeDtypeStruct(operands[0].shape, BF16)
    out = pl.pallas_call(
        functools.partial(fold_body, cut),
        out_shape=(shape,) * 4,
        in_specs=[whole()] * 8,
        out_specs=tuple([whole()] * 4),
        compiler_params=params(),
        name="fold_far",
    )(*operands)
    return (pieces[0][0], *out[:2]), (pieces[1][0], *out[2:])


def fold_near(pieces, axis):
    own, below, above = pieces
    return own, shift(below, axis, -1), shift(above, axis, 1)


def put_pieces(out, start, pieces, cut):
    size = pieces[0].shape[0]
    own, below, far_low, far_high, above = pieces
    out[start : start + size, :] = own[...]
    out[start + size : start + 2 * size, :] = below[...]
    out[start + 2 * size : start + 3 * size, :cut] = far_low[...]
    out[start + 2 * size : start + 3 * size, cut:] = far_high[...]
    out[start + 3 * size : start + 4 * size, :] = above[...]


def piece_shapes(size, width, cut):
    cols = [width, width, cut, width - cut, width]
    return [jax.ShapeDtypeStruct((size, c), BF16) for c in cols]


def pack_body(*refs):
    for half in range(2):
        out = refs[2 * SIDE + half]
        size = refs[0].shape[0]
        for index in range(SIDE):
            out[index * size : (index + 1) * size, :] = refs[SIDE * half + index][...]


def pack(first, second):
    size, width = first[0].shape
    shape = jax.ShapeDtypeStruct((SIDE * size, width), BF16)
    return pl.pallas_call(
        pack_body,
        out_shape=(shape, shape),
        in_specs=[whole()] * (2 * SIDE),
        out_specs=(whole(), whole()),
        compiler_params=params(),
        name="pack_ring",
    )(*first, *second)


def split_body(*refs):
    for half in range(2):
        own, below, above = refs[3 * half : 3 * half + 3]
        for index in range(SIDE):
            out = refs[6 + SIDE * half + index]
            size = out.shape[0]
            here = slice(index * size, (index + 1) * size)
            out[...] = own[here, :] + below[here, :] + above[here, :]


def split(first, second):
    rows, width = first[0].shape
    shape = jax.ShapeDtypeStruct((rows // SIDE, width), BF16)
    out = pl.pallas_call(
        split_body,
        out_shape=(shape,) * (2 * SIDE),
        in_specs=[whole()] * 6,
        out_specs=(whole(),) * (2 * SIDE),
        compiler_params=params(),
        name="split_ring",
    )(*first, *second)
    return out[:SIDE], out[SIDE:]


def route_body(experts, members, capacity, place_ref, ids_ref, other_ids_ref, w_ref, other_w_ref,
               pick_ref, extra_pick_ref, sent_ref, extra_sent_ref, weight_ref, extra_weight_ref, flag_ref):
    my_y, my_core, my_member = place_ref[0], place_ref[1], place_ref[2]
    tok_rows, top = ids_ref.shape
    tokens = 2 * tok_rows
    ids = jnp.concatenate([ids_ref[...], other_ids_ref[...]], axis=0)
    weights = jnp.concatenate([w_ref[...], other_w_ref[...]], axis=0).astype(F32)
    lane = lax.broadcasted_iota(jnp.int32, (tokens, experts), 1)
    group, member = div(lane, members), mod(lane, members)
    expert = (2 * group + my_core) * members + member
    named = jnp.zeros((tokens, experts), F32)
    weight = jnp.zeros((tokens, experts), F32)
    for k in range(top):
        hit = ids[:, k : k + 1] == expert
        named = jnp.where(hit, 1.0, named)
        weight = jnp.where(hit, weights[:, k : k + 1], weight)
    row = lax.broadcasted_iota(jnp.int32, (tokens, tokens), 0)
    col = lax.broadcasted_iota(jnp.int32, (tokens, tokens), 1)
    earlier = jnp.where(row > col, 1.0, 0.0).astype(BF16)
    before = dot(earlier, named.astype(BF16))

    counts = jnp.sum(named, axis=0, keepdims=True)
    lane1, group1 = lane[:1], group[:1]
    busiest = jnp.zeros((1, experts), jnp.bool_)
    for g in range(experts // members):
        inside = group1 == g
        most = jnp.max(jnp.where(inside, counts, -1.0), axis=1, keepdims=True)
        first = jnp.min(
            jnp.where(inside & (counts == most), lane1, experts), axis=1, keepdims=True
        )
        busiest = busiest | (lane1 == first)
    busy = jnp.where(busiest, 1.0, 0.0)
    lost = jnp.sum(jnp.where(before >= capacity, named * (1.0 - busy), 0.0), keepdims=True)
    mine = lane1 == my_y * members + my_member
    hot = jnp.sum(jnp.where(mine, busy, 0.0), axis=1, keepdims=True)
    flags = lax.broadcasted_iota(jnp.int32, (8, LANES), 1)
    flag_ref[...] = jnp.where(flags == 0, hot, jnp.where(flags == 1, jnp.minimum(lost, 1.0), 0.0))

    def places(total, expand, first_rank):
        slot = lax.broadcasted_iota(jnp.int32, (tokens, total), 1)
        want = (mod(slot, capacity) + first_rank).astype(F32)
        wide = lambda part: dot(part.astype(BF16), expand)
        taken = (wide(named_part) > 0.5) & (wide(before_part) == want)
        return taken, wide(weight_part)

    main = experts * capacity
    source = lax.broadcasted_iota(jnp.int32, (experts, main), 0)
    slot = lax.broadcasted_iota(jnp.int32, (experts, main), 1)
    named_part, before_part, weight_part = named, before, weight
    taken, value = places(
        main, jnp.where(div(slot, capacity) == source, 1.0, 0.0).astype(BF16), 0
    )
    picked = jnp.where(taken, 1.0, 0.0)
    pick_ref[...] = picked.astype(BF16)
    sent_ref[...] = picked.T.astype(BF16)
    weight_ref[...] = jnp.where(taken, value, 0.0).astype(BF16)

    extra = SIDE * capacity
    source = lax.broadcasted_iota(jnp.int32, (experts, extra), 0)
    slot = lax.broadcasted_iota(jnp.int32, (experts, extra), 1)
    target = div(slot, capacity) + my_y
    target = jnp.where(target >= SIDE, target - SIDE, target)
    named_part, before_part, weight_part = named * busy, before * busy, weight * busy
    taken, value = places(
        extra, jnp.where(div(source, members) == target, 1.0, 0.0).astype(BF16), capacity
    )
    picked = jnp.where(taken, 1.0, 0.0)
    extra_pick_ref[...] = picked.astype(BF16)
    extra_sent_ref[...] = picked.T.astype(BF16)
    extra_weight_ref[...] = jnp.where(taken, value, 0.0).astype(BF16)


def route(place, ids, other_ids, weights, other_weights, experts, members, capacity):
    tokens = 2 * ids.shape[0]
    main, extra = experts * capacity, SIDE * capacity
    return pl.pallas_call(
        functools.partial(route_body, experts, members, capacity),
        out_shape=(
            jax.ShapeDtypeStruct((tokens, main), BF16),
            jax.ShapeDtypeStruct((tokens, extra), BF16),
            jax.ShapeDtypeStruct((main, tokens), BF16),
            jax.ShapeDtypeStruct((extra, tokens), BF16),
            jax.ShapeDtypeStruct((tokens, main), BF16),
            jax.ShapeDtypeStruct((tokens, extra), BF16),
            jax.ShapeDtypeStruct((8, LANES), F32),
        ),
        in_specs=[pl.BlockSpec(memory_space=pltpu.SMEM)] + [whole()] * 4,
        out_specs=tuple([whole()] * 7),
        compiler_params=params(),
        name="route",
    )(place, ids, other_ids, weights, other_weights)


def dispatch_body(blocks, pick_ref, *refs):
    out_ref = refs[-1]
    half = refs[0].shape[0]
    for index in range(len(refs) // 2):
        own, other = refs[2 * index : 2 * index + 2]

        def fill(own=own, other=other):
            out_ref[...] = (
                dot(pick_ref[:, :half], own[...]) + dot(pick_ref[:, half:], other[...])
            ).astype(BF16)

        pl.when(div(pl.program_id(0), blocks) == index)(fill)


def dispatch(pick, pairs, block):
    tok_rows, width = pairs[0].shape
    slots = pick.shape[0]
    blocks = width // block
    arrays = len(pairs) // 2
    specs = []
    for index in range(arrays):
        columns = lambda i, index=index: (0, jnp.clip(i - index * blocks, 0, blocks - 1))
        specs += [pl.BlockSpec((tok_rows, block), columns)] * 2
    return pl.pallas_call(
        functools.partial(dispatch_body, blocks),
        out_shape=jax.ShapeDtypeStruct((slots, arrays * width), BF16),
        grid=(arrays * blocks,),
        in_specs=[pl.BlockSpec(pick.shape, lambda i: (0, 0))] + specs,
        out_specs=pl.BlockSpec((slots, block), lambda i: (0, i)),
        compiler_params=params(),
        cost_estimate=pl.CostEstimate(
            flops=4 * slots * tok_rows * width, bytes_accessed=4 * slots * width, transcendentals=0
        ),
        name="dispatch",
    )(pick, *pairs)


def slopes(gate, upper):
    sigma = jax.nn.sigmoid(gate)
    active = gate * sigma
    return upper * sigma * (1.0 + gate * (1.0 - sigma)), active, active * upper


def add_lanes(total_ref, here, product):
    partial = product[:, :LANES]
    for column in range(LANES, product.shape[1], LANES):
        partial = partial + product[:, column : column + LANES]
    total_ref[here, :] = jnp.where(pl.program_id(0) == 0, 0.0, total_ref[here, :]) + partial


def halves(total):
    return [slice(part * total // 2, (part + 1) * total // 2) for part in range(2)]


def extra_grads_body(cut, flag_ref, *refs):
    rows_refs, refs = refs[:10], refs[10:]
    gate_ref, up_ref, down_ref, d_gate_ref, d_up_ref, total_ref, rows = refs
    width = gate_ref.shape[0]
    keep = flag_ref[0:1, 0:1]

    @pl.when(pl.program_id(0) == 0)
    def _():
        put_pieces(rows, 0, rows_refs[:5], cut)
        put_pieces(rows, rows.shape[0] // 2, rows_refs[5:], cut)

    for here in halves(rows.shape[0]):
        slope, active, hidden = slopes(
            dot(rows[here, :width], gate_ref[...]), dot(rows[here, :width], up_ref[...])
        )
        raw = dot_t(rows[here, width:], down_ref[...]) * keep
        d_gate_ref[here, :] = (raw * slope).astype(BF16)
        d_up_ref[here, :] = (raw * active).astype(BF16)
        add_lanes(total_ref, here, raw * hidden)


def extra_grads(rows, flags, gate_mat, up_mat, down_mat, cut, block=256):
    width, hidden = gate_mat.shape
    total = rows[0].shape[0] * 2 * SIDE
    still = lambda i: (0, 0)
    return pl.pallas_call(
        functools.partial(extra_grads_body, cut),
        out_shape=(
            jax.ShapeDtypeStruct((total, hidden), BF16),
            jax.ShapeDtypeStruct((total, hidden), BF16),
            jax.ShapeDtypeStruct((total, LANES), F32),
        ),
        grid=(hidden // block,),
        in_specs=[pl.BlockSpec(flags.shape, still)]
        + [pl.BlockSpec(r.shape, still, pipeline_mode=pl.Buffered(1)) for r in rows]
        + [
            pl.BlockSpec((width, block), lambda i: (0, i)),
            pl.BlockSpec((width, block), lambda i: (0, i)),
            pl.BlockSpec((block, width), lambda i: (i, 0)),
        ],
        out_specs=(
            pl.BlockSpec((total, block), lambda i: (0, i)),
            pl.BlockSpec((total, block), lambda i: (0, i)),
            pl.BlockSpec((total, LANES), still),
        ),
        scratch_shapes=[pltpu.VMEM((total, 2 * width), BF16)],
        compiler_params=params(),
        cost_estimate=LITTLE,
        name="extra_grads",
    )(flags, *rows, gate_mat, up_mat, down_mat)


def forward_body(rows_ref, gate_ref, up_ref, slope_ref, active_ref, hidden_ref):
    for here in halves(rows_ref.shape[0]):
        rows = rows_ref[here, :]
        slope_ref[here, :], active_ref[here, :], hidden_ref[here, :] = slopes(
            dot(rows, gate_ref[...]), dot(rows, up_ref[...])
        )


def forward(rows, gate_mat, up_mat, block=256):
    width, hidden = gate_mat.shape
    total = rows.shape[0]
    state = jax.ShapeDtypeStruct((total, hidden), F32)
    columns = lambda i: (0, i)
    return pl.pallas_call(
        forward_body,
        out_shape=(state,) * 3,
        grid=(hidden // block,),
        in_specs=[
            pl.BlockSpec((total, width), lambda i: (0, 0), pipeline_mode=pl.Buffered(1)),
            pl.BlockSpec((width, block), columns),
            pl.BlockSpec((width, block), columns),
        ],
        out_specs=tuple([pl.BlockSpec((total, block), columns)] * 3),
        compiler_params=params(),
        cost_estimate=LITTLE,
        name="expert_forward",
    )(rows, gate_mat, up_mat)


def grads_body(rows_ref, down_ref, slope_ref, active_ref, hidden_ref, d_gate_ref, d_up_ref, total_ref):
    for here in halves(rows_ref.shape[0]):
        raw = dot_t(rows_ref[here, :], down_ref[...])
        d_gate_ref[here, :] = (raw * slope_ref[here, :]).astype(BF16)
        d_up_ref[here, :] = (raw * active_ref[here, :]).astype(BF16)
        add_lanes(total_ref, here, raw * hidden_ref[here, :])


def grads(rows, down_mat, slope, active, hidden_part, block=256):
    hidden, width = down_mat.shape
    total = rows.shape[0]
    columns = lambda i: (0, i)
    wide = pl.BlockSpec((total, block), columns)
    return pl.pallas_call(
        grads_body,
        out_shape=(
            jax.ShapeDtypeStruct((total, hidden), BF16),
            jax.ShapeDtypeStruct((total, hidden), BF16),
            jax.ShapeDtypeStruct((total, LANES), F32),
        ),
        grid=(hidden // block,),
        in_specs=[
            pl.BlockSpec((total, width), lambda i: (0, 0), pipeline_mode=pl.Buffered(1)),
            pl.BlockSpec((block, width), lambda i: (i, 0)),
            wide,
            wide,
            wide,
        ],
        out_specs=(wide, wide, pl.BlockSpec((total, LANES), lambda i: (0, 0))),
        compiler_params=params(),
        cost_estimate=pl.CostEstimate(
            flops=2 * total * width * hidden, bytes_accessed=24 << 20, transcendentals=0
        ),
        name="expert_grads",
    )(rows, down_mat, slope, active, hidden_part)


def contrib_body(cut, block, flag_ref, d_gate_ref, d_up_ref, total_ref, gate_ref, up_ref, *outs):
    step = pl.program_id(0)

    def tail(here):
        value = jnp.sum(total_ref[here, :], axis=1, keepdims=True)
        high = value.astype(BF16).astype(F32)
        lane = lax.broadcasted_iota(jnp.int32, (value.shape[0], LANES), 1)
        flag = jnp.where(lane == 2, flag_ref[0:1, 1:2], 0.0)
        return jnp.where(lane == 0, high, jnp.where(lane == 1, value - high, flag)).astype(BF16)

    result = (
        dot_t(d_gate_ref[...], gate_ref[...]) + dot_t(d_up_ref[...], up_ref[...])
    ).astype(BF16)
    if len(outs) == 1:
        columns = pl.ds(pl.multiple_of(step * block, block), block)
        outs[0][:, columns] = result

        @pl.when(step == 0)
        def _():
            outs[0][:, steps_width(outs[0]) :] = tail(slice(None))

        return
    size = outs[0].shape[0]
    low_steps = cut // block
    for half in range(2):
        own, below, far_low, far_high, above = outs[5 * half : 5 * half + 5]
        base = half * SIDE * size
        columns = pl.ds(pl.multiple_of(step * block, block), block)
        own[:, columns] = result[base : base + size]
        below[:, columns] = result[base + size : base + 2 * size]
        above[:, columns] = result[base + 3 * size : base + 4 * size]
        far = result[base + 2 * size : base + 3 * size]

        @pl.when(step < low_steps)
        def _():
            far_low[:, columns] = far

        @pl.when(step >= low_steps)
        def _():
            later = pl.multiple_of((step - low_steps) * block, block)
            far_high[:, pl.ds(later, block)] = far

        @pl.when(step == 0)
        def _():
            end = steps_width(own)
            own[:, end:] = tail(slice(base, base + size))
            below[:, end:] = tail(slice(base + size, base + 2 * size))
            above[:, end:] = tail(slice(base + 3 * size, base + 4 * size))
            far_high[:, end - cut :] = tail(slice(base + 2 * size, base + 3 * size))


def steps_width(ref):
    return ref.shape[1] - LANES


def contributions(flags, d_gate, d_up, total_part, gate_mat, up_mat, cut=None, block=512):
    total, hidden = d_gate.shape
    width = gate_mat.shape[0]
    if cut is None:
        shapes = [jax.ShapeDtypeStruct((total, width + LANES), BF16)]
    else:
        shapes = piece_shapes(total // (2 * SIDE), width + LANES, cut) * 2
    still = lambda i: (0, 0)
    out = pl.pallas_call(
        functools.partial(contrib_body, cut, block),
        out_shape=tuple(shapes),
        grid=(width // block,),
        in_specs=[
            pl.BlockSpec(flags.shape, still),
            pl.BlockSpec((total, hidden), still),
            pl.BlockSpec((total, hidden), still),
            pl.BlockSpec((total, LANES), still),
            pl.BlockSpec((block, hidden), lambda i: (i, 0)),
            pl.BlockSpec((block, hidden), lambda i: (i, 0)),
        ],
        out_specs=tuple(pl.BlockSpec(s.shape, still) for s in shapes),
        compiler_params=params(),
        cost_estimate=LITTLE
        if cut
        else pl.CostEstimate(
            flops=4 * total * width * hidden, bytes_accessed=40 << 20, transcendentals=0
        ),
        name="expert_contributions",
    )(flags, d_gate, d_up, total_part, gate_mat, up_mat)
    return out[0] if cut is None else (out[:5], out[5:])


def choices_body(members, capacity, place_ref, ids_ref, other_ids_ref, pick_ref, extra_pick_ref,
                 *outs):
    my_y, my_core = place_ref[0], place_ref[1]
    ids = jnp.concatenate([ids_ref[...], other_ids_ref[...]], axis=0)
    tokens, top = ids.shape
    slot = div(lax.broadcasted_iota(jnp.int32, pick_ref.shape, 1), capacity)
    group, member = div(slot, members), mod(slot, members)
    expert = (2 * group + my_core) * members + member
    far_y = div(lax.broadcasted_iota(jnp.int32, extra_pick_ref.shape, 1), capacity) + my_y
    far_y = jnp.where(far_y >= SIDE, far_y - SIDE, far_y)
    far_group = 2 * far_y + my_core
    picked = pick_ref[...].astype(F32)
    extra_picked = extra_pick_ref[...].astype(F32)
    half = tokens // 2
    for k in range(top):
        here = slice(k * half, (k + 1) * half)
        name = ids[:, k : k + 1]
        hit = jnp.where(name == expert, picked, 0.0)
        placed = jnp.sum(hit, axis=1, keepdims=True)
        extra_hit = jnp.where(div(name, members) == far_group, extra_picked, 0.0)
        extra_hit = jnp.where(placed > 0.5, 0.0, extra_hit)
        outs[0][here, :] = hit[:half].astype(BF16)
        outs[1][here, :] = extra_hit[:half].astype(BF16)
        outs[2][here, :] = hit[half:].astype(BF16)
        outs[3][here, :] = extra_hit[half:].astype(BF16)


def choices(place, ids, other_ids, pick, extra_pick, members, capacity):
    rows = ids.shape[0] * ids.shape[1]
    shapes = [jax.ShapeDtypeStruct((rows, p.shape[1]), BF16) for p in (pick, extra_pick)]
    return pl.pallas_call(
        functools.partial(choices_body, members, capacity),
        out_shape=tuple(shapes * 2),
        in_specs=[pl.BlockSpec(memory_space=pltpu.SMEM)] + [whole()] * 4,
        out_specs=(whole(),) * 4,
        compiler_params=params(),
        cost_estimate=LITTLE,
        name="choices",
    )(place, ids, other_ids, pick, extra_pick)


def choice_sums(top, tokens, hit_ref, extra_hit_ref, tail_ref, extra_tail_ref):
    tail = tail_ref[...]
    value = dot(hit_ref[...], tail) + dot(extra_hit_ref[...], extra_tail_ref[...])
    flags = tail.astype(F32)
    flag_lane = lax.broadcasted_iota(jnp.int32, flags.shape, 1)
    flag = jnp.max(jnp.where(flag_lane == 2, flags, 0.0), keepdims=True)
    lane = lax.broadcasted_iota(jnp.int32, (tokens, LANES), 1)
    out = jnp.where(lane == top, flag, 0.0)
    for k in range(top):
        part = value[tokens * k : tokens * (k + 1)]
        found = jnp.sum(jnp.where(lane < 2, part, 0.0), axis=1, keepdims=True)
        out = jnp.where(lane == k, found, out)
    return out


def combine_specs(half, weight, extra_weight, hit, extra_hit, width, block, columns):
    still = lambda *_: (0, 0)
    mine = lambda *_: (half, 0)
    tail = lambda *_: (0, width // LANES)
    tokens, main = weight.shape[0] // 2, weight.shape[1]
    rest = extra_weight.shape[1]
    return [
        pl.BlockSpec((tokens, main), mine),
        pl.BlockSpec((tokens, rest), mine),
        pl.BlockSpec(hit.shape, still),
        pl.BlockSpec(extra_hit.shape, still),
        pl.BlockSpec((main, block), columns),
        pl.BlockSpec((rest, block), columns),
        pl.BlockSpec((main, LANES), tail),
        pl.BlockSpec((rest, LANES), tail),
    ]


def send_body(top, weight_ref, extra_weight_ref, hit_ref, extra_hit_ref, back_ref, extra_ref,
              tail_ref, extra_tail_ref, sum_ref, route_ref):
    total = dot(weight_ref[...], back_ref[...]) + dot(extra_weight_ref[...], extra_ref[...])
    sum_ref[...] = total.astype(BF16)

    @pl.when(pl.program_id(0) == 0)
    def _():
        route_ref[...] = choice_sums(
            top, sum_ref.shape[0], hit_ref, extra_hit_ref, tail_ref, extra_tail_ref
        )


def combine_other(weight, extra_weight, hit, extra_hit, back, extra, block=1792):
    tokens = weight.shape[0] // 2
    width = back.shape[1] - LANES
    columns = lambda i: (0, i)
    return pl.pallas_call(
        functools.partial(send_body, hit.shape[0] // tokens),
        out_shape=(
            jax.ShapeDtypeStruct((tokens, width), BF16),
            jax.ShapeDtypeStruct((tokens, LANES), F32),
        ),
        grid=(width // block,),
        in_specs=combine_specs(1, weight, extra_weight, hit, extra_hit, width, block, columns),
        out_specs=(
            pl.BlockSpec((tokens, block), columns),
            pl.BlockSpec((tokens, LANES), lambda i: (0, 0)),
        ),
        compiler_params=params(),
        name="combine_other",
    )(weight, extra_weight, hit, extra_hit, back, extra, back, extra)


def combine_body(top, weight_ref, extra_weight_ref, hit_ref, extra_hit_ref, back_ref, extra_ref,
                 tail_ref, extra_tail_ref, other_ref, other_route_ref, x_grad_ref, route_ref):
    total = dot(weight_ref[...], back_ref[...]) + dot(extra_weight_ref[...], extra_ref[...])
    x_grad_ref[...] = (total + other_ref[...].astype(F32)).astype(BF16)

    @pl.when(pl.program_id(0) == 0)
    def _():
        route_ref[...] = other_route_ref[...] + choice_sums(
            top, total.shape[0], hit_ref, extra_hit_ref, tail_ref, extra_tail_ref
        )


def combine(weight, extra_weight, hit, extra_hit, back, extra, other_sums, other_routes, block=1792):
    tokens, width = other_sums.shape
    columns = lambda i: (0, i)
    still = lambda i: (0, 0)
    wide = pl.BlockSpec((tokens, block), columns)
    narrow = pl.BlockSpec((tokens, LANES), still)
    return pl.pallas_call(
        functools.partial(combine_body, hit.shape[0] // tokens),
        out_shape=(
            jax.ShapeDtypeStruct((tokens, width), BF16),
            jax.ShapeDtypeStruct((tokens, LANES), F32),
        ),
        grid=(width // block,),
        in_specs=combine_specs(0, weight, extra_weight, hit, extra_hit, width, block, columns)
        + [wide, narrow],
        out_specs=(wide, narrow),
        compiler_params=params(),
        name="combine",
    )(weight, extra_weight, hit, extra_hit, back, extra, back, extra, other_sums, other_routes)


def padded_path(tokens, out_grad, route_weights, expert_ids, gate_mat, up_mat, down_mat):
    tok_rows, width = tokens.shape
    top = expert_ids.shape[1]
    experts = lax.axis_size(ALL)
    capacity = 2 * tok_rows * top // experts
    named = jnp.any(expert_ids[:, :, None] == jnp.arange(experts, dtype=jnp.int32), axis=1)
    place = jnp.arange(tok_rows, dtype=jnp.int32)
    earlier = (place[:, None] > place[None, :]).astype(BF16)
    before = dot(earlier, named.astype(BF16)).astype(jnp.int32)
    slots = expert_ids * capacity + jnp.take_along_axis(before, expert_ids, axis=1)
    slot_iota = jnp.arange(experts * capacity, dtype=jnp.int32)
    taken = slots[:, :, None] == slot_iota[None, None, :]
    pick = jnp.any(taken, axis=1).astype(BF16)
    rows_x = exchange(dot_tl(pick, tokens).astype(BF16), ALL)
    rows_dy = exchange(dot_tl(pick, out_grad).astype(BF16), ALL)
    gate = dot(rows_x, gate_mat)
    upper = dot(rows_x, up_mat)
    sigma = jax.nn.sigmoid(gate)
    active = gate * sigma
    raw = dot_t(rows_dy, down_mat)
    routes = exchange(jnp.sum(raw * (active * upper), axis=1), ALL)
    d_gate = (raw * (upper * sigma * (1.0 + gate * (1.0 - sigma)))).astype(BF16)
    d_up = (raw * active).astype(BF16)
    back = exchange((dot_t(d_gate, gate_mat) + dot_t(d_up, up_mat)).astype(BF16), ALL)
    weights = jnp.sum(jnp.where(taken, route_weights[:, :, None], jnp.zeros((), BF16)), axis=1)
    x_grad = dot(weights, back).astype(BF16)
    return x_grad, jnp.sum(jnp.where(taken, routes[None, None, :], 0.0), axis=2)


def local(tokens, out_grad, route_weights, expert_ids, w_gate, w_up, w_down):
    tok_rows, width = tokens.shape
    top = expert_ids.shape[1]
    members = lax.axis_size("ingrp")
    experts = lax.axis_size(LIKE)
    capacity = tok_rows * top // experts
    main = experts * capacity
    mats = (w_gate[0], w_up[0], w_down[0])
    place = jnp.stack([lax.axis_index(name) for name in ALL]).astype(jnp.int32)

    other_ids, other_weights = swap(expert_ids), swap(route_weights)
    other_tokens, other_out_grad = swap(tokens), swap(out_grad)
    pick, extra_pick, sent_pick, extra_sent_pick, weight, extra_weight, flags = route(
        place, expert_ids, other_ids, route_weights, other_weights, experts, members, capacity
    )
    pair_x, pair_dy = (tokens, other_tokens), (out_grad, other_out_grad)

    cut, back_cut = width, 3 * 512
    extra = dispatch(extra_sent_pick, pair_x + pair_dy, 3584)
    parts = [extra[i * capacity : (i + 1) * capacity] for i in range(SIDE)]
    parts = parts[:1] + [shift_y(parts[i], i) for i in range(1, SIDE)]
    sent_x = dispatch(sent_pick, pair_x, 1792)
    sent_x, *parts = lax.optimization_barrier((sent_x, *parts))
    first = short_gather(jnp.concatenate(parts[:2], axis=0), 0)
    second = short_gather(jnp.concatenate(parts[2:], axis=0), 1)
    sent_x, first, second = lax.optimization_barrier((sent_x, first, second))
    rows_x = exchange(sent_x, LIKE)

    first, second = pack(first, second)
    sent_dy = dispatch(sent_pick, pair_dy, 1792)
    hits = choices(place, expert_ids, other_ids, pick, extra_pick, members, capacity)
    first, second, sent_dy, hits = lax.optimization_barrier((first, second, sent_dy, hits))
    first, second = near_gather(first, 1), near_gather(second, 0)
    state = forward(rows_x, *mats[:2])
    state, sent_dy, first, second = lax.optimization_barrier((state, sent_dy, first, second))
    first, second = far_gather(first, 1, cut), far_gather(second, 0, cut)
    sent_dy, first, second = lax.optimization_barrier((sent_dy, first, second))
    rows_dy = exchange(sent_dy, LIKE)

    first, second = contributions(
        flags, *extra_grads(first + second, flags, *mats, cut), *mats[:2], back_cut
    )
    first, second = fold_far((first, second), (1, 0), back_cut)
    rows_dy, first, second = lax.optimization_barrier((rows_dy, first, second))
    first, second = fold_near(first, 1), fold_near(second, 0)
    state = grads(rows_dy, mats[2], *state)
    first, second = split(first, second)
    state, first, second = lax.optimization_barrier((state, first, second))
    first, second = short_return(first, 0), short_return(second, 1)
    result = contributions(flags, *state, *mats[:2])
    result, first, second = lax.optimization_barrier((result, first, second))
    back = exchange(result, LIKE)
    first, second = sum(first[1:], first[0]), sum(second[1:], second[0])
    parts = [first[:capacity], first[capacity:], second[:capacity], second[capacity:]]
    parts = parts[:1] + [shift_y(parts[i], -i) for i in range(1, SIDE)]
    extra_back = jnp.concatenate(parts, axis=0)

    weights = (weight, extra_weight)
    other_sums, other_routes = combine_other(*weights, *hits[2:], back, extra_back)
    x_grad, routes = combine(
        *weights, *hits[:2], back, extra_back, swap(other_sums), swap(other_routes)
    )
    return lax.cond(
        routes[0, top] > 0,
        lambda: padded_path(tokens, out_grad, route_weights, expert_ids, *mats),
        lambda: (x_grad, routes[:, :top]),
    )


def solution(mesh):
    devices = mesh.devices
    split_mesh = Mesh(devices.reshape(devices.shape[0] // 2, 2, devices.shape[1]), ALL)
    rows = P(ALL, None)
    mats = P(ALL, None, None)
    return jax.shard_map(
        local,
        mesh=split_mesh,
        in_specs=(rows, rows, rows, rows, mats, mats, mats),
        out_specs=(rows, rows),
        check_vma=False,
    )
```
